512 devices in a mesh: ulysses: 8 (over y_lo, core), blk: 64 (over x, z, y_hi).
Axes of the slice: x: 4, y: 8 (y_hi: 2, y_lo: 4; y = y_hi * 4 + y_lo), z: 8, core: 2. Of those that a mesh axis runs over, the one named last changes fastest.
Arguments:
- query_first: bfloat16 [128, 64, 8, 128], P('blk', None, 'ulysses'), may hold values from -6 to 6
- query_second: bfloat16 [128, 64, 8, 128], P('blk', None, 'ulysses'), may hold values from -6 to 6
- key_first: bfloat16 [128, 64, 8, 128], P('blk', None, 'ulysses'), may hold values from -6 to 6
- key_second: bfloat16 [128, 64, 8, 128], P('blk', None, 'ulysses'), may hold values from -6 to 6
- values: bfloat16 [128, 64, 8, 256], P('blk', None, 'ulysses'), may hold values from -6 to 6
- out_first: bfloat16 [128, 64, 8, 256], P('blk', None, 'ulysses'), may hold values from -6 to 6, as said below
- out_second: bfloat16 [128, 64, 8, 256], P('blk', None, 'ulysses'), may hold values from -6 to 6, as said below
- log_totals: float32 [8, 2, 128, 64], P('ulysses', None, 'blk'), as said below
- lambdas: float32 [8], P('ulysses'), may hold values from 0.1 to 0.8
- norm_gain: float32 [8, 256], P('ulysses'), may hold values from 0.1 to 1.9
- cotangent: bfloat16 [128, 64, 8, 256], P('blk', 'ulysses'), may hold values from -6 to 6
- block_of: int32 [128], replicated, may hold values from 0 to 127, as said below
Outputs:
- grad_query_first: bfloat16 [128, 64, 8, 128], P('blk', None, 'ulysses')
- grad_query_second: bfloat16 [128, 64, 8, 128], P('blk', None, 'ulysses')
- grad_key_first: bfloat16 [128, 64, 8, 128], P('blk', None, 'ulysses')
- grad_key_second: bfloat16 [128, 64, 8, 128], P('blk', None, 'ulysses')
- grad_values: bfloat16 [128, 64, 8, 256], P('blk', None, 'ulysses')
The draws below stay inside these ranges and needn't reach their ends.
Inputs may be any that keep to these rules, and one draw needn't show every extreme that they name: `block_of`: slots 2d and 2d + 1 hold blocks c_d and 127 - c_d, where c_0 to c_last form a permutation of 0 to 63. `out_first`: the causal softmax average of values under the first pair's scaled scores, normalised over visible keys, rounded to bfloat16. `out_second`: likewise for the second pair. log_totals[h, 0] and log_totals[h, 1] are the logarithms of the sums over visible keys of exp of the first and second pair's scaled scores.
All inputs are finite; a program needn't handle non-finite values.
Results may differ from the reference program's by a relative error of at most 0.0085.
Values may be sent and summed in bfloat16 or wider, within the bound.
A program may use at most 64 MiB of HBM per device.

```python
import math
import jax
import jax.numpy as jnp
from jax import lax

DH = 128
DV = 256
BLOCK = 64
HEADS = 8
N_BLK = 64


def paired_table(key):
    lower_block = jax.random.permutation(jax.random.fold_in(key, 11), N_BLK).astype(jnp.int32)
    upper_block = 2 * N_BLK - 1 - lower_block
    return jnp.stack([lower_block, upper_block], axis=1).reshape(2 * N_BLK)


def random_rows(key, label_id, feature_width):
    branch_key = jax.random.fold_in(key, label_id)
    shape_all = (2 * N_BLK, BLOCK, HEADS, feature_width)
    drawn_rows = jax.random.truncated_normal(jax.random.fold_in(branch_key, 1), -6.0, 6.0, shape_all, jnp.float32)
    return drawn_rows.astype(jnp.bfloat16)


def forward_pass(key, query_label, key_label):
    total_rows = 2 * N_BLK * BLOCK
    positions = (paired_table(key)[:, None] * BLOCK + jnp.arange(BLOCK, dtype=jnp.int32)[None, :]).reshape(total_rows)

    def heads_first(member):
        return jnp.transpose(member.reshape(total_rows, HEADS, member.shape[3]), (1, 0, 2)).astype(jnp.float32)
    queries = heads_first(random_rows(key, query_label, DH))
    keys_all = heads_first(random_rows(key, key_label, DH))
    values_all = heads_first(random_rows(key, 5, DV))
    tile_rows = min(512, total_rows)
    starts = jnp.arange(0, total_rows, tile_rows)

    def per_head(head_in):
        head_query, head_key, head_value = head_in

        def per_block(first_row):
            block_query = lax.dynamic_slice_in_dim(head_query, first_row, tile_rows, 0)
            block_pos = lax.dynamic_slice_in_dim(positions, first_row, tile_rows, 0)
            scores = jnp.dot(block_query, head_key.T, precision=lax.Precision.HIGHEST) / math.sqrt(DH)
            scores = jnp.where(positions[None, :] <= block_pos[:, None], scores, -jnp.inf)
            largest = jnp.max(scores, axis=1, keepdims=True)
            weights = jnp.exp(scores - largest)
            weight_sum = jnp.sum(weights, axis=1, keepdims=True)
            log_total = (largest + jnp.log(weight_sum))[:, 0]
            mixed_rows = jnp.dot(weights / weight_sum, head_value, precision=lax.Precision.HIGHEST)
            return (log_total, mixed_rows)
        log_total, mixed_rows = lax.map(per_block, starts)
        return (log_total.reshape(total_rows), mixed_rows.reshape(total_rows, DV))
    return lax.map(per_head, (queries, keys_all, values_all))


def rows_first(mixed_rows):
    return jnp.transpose(mixed_rows, (1, 0, 2)).reshape(2 * N_BLK, BLOCK, HEADS, DV).astype(jnp.bfloat16)


def draw_query_first(key, part):
    return random_rows(key, 1, DH)


def draw_query_second(key, part):
    return random_rows(key, 2, DH)


def draw_key_first(key, part):
    return random_rows(key, 3, DH)


def draw_key_second(key, part):
    return random_rows(key, 4, DH)


def draw_values(key, part):
    return random_rows(key, 5, DV)


def draw_out_first(key, part):
    log_total, mixed_rows = forward_pass(key, 1, 3)
    return rows_first(mixed_rows)


def draw_out_second(key, part):
    log_total, mixed_rows = forward_pass(key, 2, 4)
    return rows_first(mixed_rows)


def draw_log_totals(key, part):
    total_one, unused_one = forward_pass(key, 1, 3)
    total_two, unused_two = forward_pass(key, 2, 4)
    return jnp.stack([total_one, total_two], axis=1).reshape(HEADS, 2, 2 * N_BLK, BLOCK)


def draw_block_of(key, part):
    return paired_table(key)


def block_scale(own_key, extent, pieces, least, high):
    gain, own = 1.0, jax.random.fold_in(own_key, 6)
    for axis_at, blocks in pieces:
        heights = jnp.exp(jax.random.uniform(jax.random.fold_in(own, axis_at), (blocks,), jnp.float32, least / len(pieces), high / len(pieces)))
        gain = gain * jnp.repeat(heights, extent[axis_at] // blocks).reshape([-1 if axis == axis_at else 1 for axis in range(len(extent))])
    return gain


def bell_draw(key, shape, spread, most, pieces=(), held_as=jnp.bfloat16):
    array = jax.random.normal(key, shape, jnp.float32) * spread
    if len(pieces) > 0:
        array = block_scale(key, shape, pieces, -0.22, 0.18) * array
    return jnp.clip(array, min=-most, max=most).astype(held_as)


def setup_inputs(seed: int = 0) -> dict:
    seeds = jax.random.split(jax.random.key(seed), 13)
    query_first = draw_query_first(jax.random.fold_in(seeds[12], 71), 0)
    query_second = draw_query_second(jax.random.fold_in(seeds[12], 71), 0)
    key_first = draw_key_first(jax.random.fold_in(seeds[12], 71), 0)
    key_second = draw_key_second(jax.random.fold_in(seeds[12], 71), 0)
    values = draw_values(jax.random.fold_in(seeds[12], 71), 0)
    out_first = draw_out_first(jax.random.fold_in(seeds[12], 71), 0)
    out_second = draw_out_second(jax.random.fold_in(seeds[12], 71), 0)
    log_totals = draw_log_totals(jax.random.fold_in(seeds[12], 71), 0)
    lambdas = jnp.clip(jnp.exp(math.log(0.8) - 2.0794415 * jax.random.uniform(seeds[8], (HEADS,), jnp.float32) ** block_scale(seeds[8], (HEADS,), ((0, 8),), -0.2, 0.2)), 0.1, 0.8)
    norm_gain = jnp.clip(1.0 + 0.18 * jax.random.normal(seeds[9], (HEADS, DV), jnp.float32), 0.1, 1.9)
    cotangent = bell_draw(seeds[10], (2 * N_BLK, BLOCK, HEADS, DV), 1.0, 6.0, ((0, 64), (1, 8)))
    block_of = draw_block_of(jax.random.fold_in(seeds[12], 71), 0)
    return dict(query_first=query_first, query_second=query_second, key_first=key_first, key_second=key_second, values=values, out_first=out_first, out_second=out_second, log_totals=log_totals, lambdas=lambdas, norm_gain=norm_gain, cotangent=cotangent, block_of=block_of)


norm_eps = 1e-05

def head_backward(inputs_all, positions, scale_qk, tile_rows):
    first_query, second_query, first_key, second_key, values, grad_out, head_stats, lambda_one = inputs_all
    total_rows = first_query.shape[0]
    block_count = total_rows // tile_rows

    def blocks(member):
        return member.reshape((block_count, tile_rows) + member.shape[1:])

    def one_block(running, block_in):
        key_one, key_two, value_sum = running
        block_first, block_second, block_grad, block_stats, block_pos = block_in
        visible = positions[None, :] <= block_pos[:, None]
        score_one = jnp.dot(block_first, first_key.T, preferred_element_type=jnp.float32) * scale_qk
        score_two = jnp.dot(block_second, second_key.T, preferred_element_type=jnp.float32) * scale_qk
        prob_one = jnp.exp(jnp.where(visible, score_one - block_stats[0][:, None], -jnp.inf))
        prob_two = jnp.exp(jnp.where(visible, score_two - block_stats[1][:, None], -jnp.inf))
        grad_attn = jnp.dot(block_grad, values.T, preferred_element_type=jnp.float32)
        grad_one = (prob_one * (grad_attn - block_stats[2][:, None])).astype(jnp.bfloat16)
        grad_two = (-lambda_one * prob_two * (grad_attn - block_stats[3][:, None])).astype(jnp.bfloat16)
        weights = (prob_one - lambda_one * prob_two).astype(jnp.bfloat16)
        query_one = (jnp.dot(grad_one, first_key, preferred_element_type=jnp.float32) * scale_qk).astype(jnp.bfloat16)
        query_two = (jnp.dot(grad_two, second_key, preferred_element_type=jnp.float32) * scale_qk).astype(jnp.bfloat16)
        key_one = key_one + jnp.dot(grad_one.T, block_first, preferred_element_type=jnp.float32)
        key_two = key_two + jnp.dot(grad_two.T, block_second, preferred_element_type=jnp.float32)
        value_sum = value_sum + jnp.dot(weights.T, block_grad, preferred_element_type=jnp.float32)
        return ((key_one, key_two, value_sum), (query_one, query_two))
    stats_blocks = jnp.transpose(head_stats.reshape(4, block_count, tile_rows), (1, 0, 2))
    zero_key = jnp.zeros((total_rows, first_key.shape[1]), jnp.float32)
    zero_value = jnp.zeros((total_rows, values.shape[1]), jnp.float32)
    finals, query_parts = lax.scan(one_block, (zero_key, zero_key, zero_value), (blocks(first_query), blocks(second_query), blocks(grad_out), stats_blocks, blocks(positions)))
    return (query_parts[0].reshape(total_rows, first_key.shape[1]), query_parts[1].reshape(total_rows, first_key.shape[1]), (finals[0] * scale_qk).astype(jnp.bfloat16), (finals[1] * scale_qk).astype(jnp.bfloat16), finals[2].astype(jnp.bfloat16))

def reference(query_first, query_second, key_first, key_second, values, out_first, out_second, log_totals, lambdas, norm_gain, cotangent, block_of):
    slot_count, block_len, head_count, key_width = query_first.shape
    total_rows = slot_count * block_len
    scale_qk = 1.0 / math.sqrt(key_width)
    positions = (block_of[:, None] * block_len + jnp.arange(block_len, dtype=jnp.int32)[None, :]).reshape(total_rows).astype(jnp.int32)
    first_out = out_first.astype(jnp.float32)
    second_out = out_second.astype(jnp.float32)
    combined = first_out - lambdas[None, None, :, None] * second_out
    inv_rms = lax.rsqrt(lax.optimization_barrier(jnp.mean(combined * combined, axis=-1, keepdims=True)) + norm_eps)
    gained = norm_gain[None, None] * cotangent.astype(jnp.float32)
    centre = lax.optimization_barrier(jnp.mean(combined * gained, axis=-1, keepdims=True))
    grad_out = (inv_rms * (gained - combined * inv_rms * inv_rms * centre)).astype(jnp.bfloat16)
    grad_wide = grad_out.astype(jnp.float32)
    dot_one = lax.optimization_barrier(jnp.sum(grad_wide * first_out, axis=-1)).reshape(total_rows, head_count).T
    dot_two = lax.optimization_barrier(jnp.sum(grad_wide * second_out, axis=-1)).reshape(total_rows, head_count).T
    head_stats = jnp.concatenate([log_totals.reshape(head_count, 2, total_rows), dot_one[:, None], dot_two[:, None]], axis=1)

    def heads_first(member):
        return jnp.transpose(member.reshape((total_rows, head_count) + member.shape[3:]), (1, 0, 2))
    tile_rows = min(512, total_rows)
    results = lax.map(lambda inputs_all: head_backward(inputs_all, positions, scale_qk, tile_rows), (heads_first(query_first), heads_first(query_second), heads_first(key_first), heads_first(key_second), heads_first(values), heads_first(grad_out), head_stats, lambdas))

    def rows_first(member):
        return jnp.transpose(member, (1, 0, 2)).reshape((slot_count, block_len, head_count, member.shape[2]))
    return (rows_first(results[0]), rows_first(results[1]), rows_first(results[2]), rows_first(results[3]), rows_first(results[4]))
```

```python
import functools
import math

import jax
import jax.numpy as jnp
from jax import lax
from jax.experimental import pallas as pl
from jax.experimental.pallas import tpu as pltpu
from jax.sharding import PartitionSpec as P

MESH = pl.DeviceIdType.MESH
NX, NZ, NY, NU = 4, 8, 2, 8
ROWS, DH, DV, HALF = 128, 128, 256, 64
GROWS = ROWS + 16
EPS = 1e-05
LOG2E = math.log2(math.e)
F32, BF16 = jnp.float32, jnp.bfloat16
KSLOT = {4: 0, 5: 1, 3: 2, 6: 3, 2: 4, 7: 5, 1: 6, 0: 7}
KFROM = {place: d for d, place in KSLOT.items()}


def qslot(dx, dy):
    return dx + (0 if dy else 4)


def dot(a, b, dims):
    return lax.dot_general(a, b, (dims, ((), ())), preferred_element_type=F32)


def split3(value):
    high = value.astype(BF16)
    rest = value - high.astype(F32)
    middle = rest.astype(BF16)
    low = (rest - middle.astype(F32)).astype(BF16)
    return high.astype(F32), middle.astype(F32), low.astype(F32)


def kernel(
    q1, q2, k1, k2, v, o1, o2, totals, lam_ref, gain, cot, block_of,
    gq1, gq2, gk1, gk2, gv,
    cot_out, cot_in, qb, gb, kb, vb, stat, qpos, gq_sum, gk_sum, gv_sum,
    zs, zr, xs, xr, ys, yr, send, recv,
):
    u = lax.axis_index("ulysses")
    blk = lax.axis_index("blk")
    x, z, y = blk // (NZ * NY), (blk // NY) % NZ, blk % NY

    def at(nx, nz, ny):
        return {"blk": (lax.rem(nx, NX) * NZ + lax.rem(nz, NZ)) * NY + lax.rem(ny, NY)}

    up, down, across = at(x, z + 1, y), at(x, z + NZ - 1, y), at(x, z, y + 1)
    x_peers = {dx: at(x + dx, z, y) for dx in range(1, NX)}
    u_peers = {r: {"ulysses": lax.rem(u + r, NU)} for r in range(1, NU)}
    started = []

    def copy(name, src, dst, device):
        i = names.setdefault(name, len(names))
        return pltpu.make_async_remote_copy(
            src_ref=src, dst_ref=dst, send_sem=send.at[i], recv_sem=recv.at[i],
            device_id=device, device_id_type=MESH,
        )

    names = {}
    moves = {}

    def go(name, src, dst, device):
        move = copy(name, src, dst, device)
        move.start()
        moves[name] = move

    def arrived(name):
        moves[name].wait_recv()

    barrier = pltpu.get_barrier_semaphore()
    partners = [up, down, across, *x_peers.values(), *u_peers.values()]
    for partner in partners:
        pl.semaphore_signal(barrier, inc=1, device_id=partner, device_id_type=MESH)

    own_q, own_k = qslot(0, 0), KSLOT[0]
    qb[own_q, :, :DH] = q1[...]
    qb[own_q, :, DH:] = q2[...]
    kb[own_k, :, :DH] = k1[...]
    kb[own_k, :, DH:] = k2[...]
    vb[own_k] = v[...]
    to_row = lax.broadcasted_iota(jnp.int32, (ROWS, ROWS), 0)
    from_row = lax.broadcasted_iota(jnp.int32, (ROWS, ROWS), 1)
    wanted = (to_row % 16) * 8 + to_row // 16
    order = jnp.where(from_row == wanted, 1.0, 0.0).astype(BF16)
    rows_in = cot[...].astype(F32).reshape(ROWS, DV).astype(BF16)
    by_head = dot(order, rows_in, ((1,), (0,))).astype(BF16).reshape(NU, 16, DV)
    cot_out[...] = by_head

    pl.semaphore_wait(barrier, len(partners))

    for r, device in u_peers.items():
        go(f"c{r}", cot_out.at[lax.rem(u + r, NU)], cot_in.at[u], device)
    for way, device, sign in (("u", up, 1), ("d", down, -1)):
        slot = KSLOT[sign % NZ]
        go(f"k{way}1", kb.at[own_k], kb.at[slot], device)
        go(f"v{way}1", vb.at[own_k], vb.at[slot], device)
    go("qy", qb.at[own_q], qb.at[qslot(0, 1)], across)
    for dx, device in x_peers.items():
        go(f"q{dx}", qb.at[own_q], qb.at[qslot(dx, 0)], device)

    cot_in[u] = cot_out[u]
    for r in u_peers:
        arrived(f"c{r}")
    lam = lam_ref[0]
    parts = cot_in[...].astype(F32)
    grad_y = jnp.concatenate(
        [parts[w, s * 8 : s * 8 + 8] for s in range(2) for w in range(NU)], axis=0
    )
    first_out, second_out = o1[...].astype(F32), o2[...].astype(F32)
    combined = first_out - lam * second_out
    inv_rms = lax.rsqrt(jnp.mean(combined * combined, axis=-1, keepdims=True) + EPS)
    gained = gain[...] * grad_y
    centre = jnp.mean(combined * gained, axis=-1, keepdims=True)
    grad_out = (inv_rms * (gained - combined * inv_rms * inv_rms * centre)).astype(BF16)
    gb[own_q, :ROWS] = grad_out
    wide = grad_out.astype(F32)
    dot_one = jnp.sum(wide * first_out, axis=-1, keepdims=True)
    dot_two = jnp.sum(wide * second_out, axis=-1, keepdims=True)
    row_one = jnp.broadcast_to(dot_one, (ROWS, ROWS)).T[:1]
    row_two = jnp.broadcast_to(dot_two, (ROWS, ROWS)).T[:1]
    log_lam = jnp.log2(jnp.full((1, ROWS), lam, F32))
    total_one = jnp.concatenate([totals[0, 0, :1], totals[0, 0, 1:]], axis=1) * LOG2E
    total_two = jnp.concatenate([totals[0, 1, :1], totals[0, 1, 1:]], axis=1) * LOG2E
    stats = jnp.concatenate([total_one, total_two - log_lam, row_one, row_two], axis=0)
    coded = jnp.concatenate([*split3(stats), jnp.zeros((4, ROWS), F32)], axis=0)
    gb[own_q, ROWS:] = jnp.concatenate([coded, jnp.zeros((16, ROWS), F32)], axis=1).astype(BF16)

    go("gy", gb.at[own_q], gb.at[qslot(0, 1)], across)
    for dx, device in x_peers.items():
        go(f"g{dx}", gb.at[own_q], gb.at[qslot(dx, 0)], device)

    def pass_on(hop, kinds):
        for kind, way, device, sign in kinds:
            arrived(f"{kind}{way}{hop}")
            held = {"k": kb, "v": vb}[kind]
            here, there = KSLOT[sign * hop % NZ], KSLOT[sign * (hop + 1) % NZ]
            go(f"{kind}{way}{hop + 1}", held.at[here], held.at[there], device)

    both = [(kind, way, device, sign) for way, device, sign in (("u", up, 1), ("d", down, -1)) for kind in "kv"]
    pass_on(1, both)
    arrived("qy")
    for dx, device in x_peers.items():
        go(f"p{dx}", qb.at[qslot(0, 1)], qb.at[qslot(dx, 1)], device)
    pass_on(2, both)
    arrived("gy")
    for dx, device in x_peers.items():
        go(f"h{dx}", gb.at[qslot(0, 1)], gb.at[qslot(dx, 1)], device)
    pass_on(3, [both[0], both[3]])
    arrived("vu3")
    arrived("kd3")
    arrived("ku4")
    arrived("vd4")
    for dx in x_peers:
        for name in "qpgh":
            arrived(f"{name}{dx}")

    lane = lax.broadcasted_iota(jnp.int32, (8, ROWS), 1)
    for dy in range(NY):
        for dx in range(NX):
            slot = qslot(dx, dy)
            source = at(x + NX - dx, z, y + dy)["blk"]
            coded = gb[slot, ROWS:, :ROWS].astype(F32)
            c, part = slot // 2, pl.ds(slot % 2 * ROWS, ROWS)
            stat[c, 0:4, part] = coded[0:4] + coded[4:8] + coded[8:12]
            low, high = block_of[2 * source], block_of[2 * source + 1]
            qpos[c, :, part] = jnp.where(lane < HALF, low * HALF + lane, high * HALF + lane - HALF)
    gq_sum[...] = jnp.zeros_like(gq_sum)
    scale = 1.0 / math.sqrt(DH)
    row = lax.broadcasted_iota(jnp.int32, (2 * ROWS, 1), 0)

    def tile(p):
        places = []
        for slot in (2 * p, 2 * p + 1):
            source = at(x, z + NZ - KFROM[slot], y)["blk"]
            places += [block_of[2 * source], block_of[2 * source + 1]]
        start = jnp.where(
            row < ROWS,
            jnp.where(row < HALF, places[0], places[1]),
            jnp.where(row < ROWS + HALF, places[2], places[3]),
        )
        kpos = start * HALF + row % HALF
        gk_sum[p] = jnp.zeros((2 * ROWS, 2 * DH), F32)
        gv_sum[p] = jnp.zeros((2 * ROWS, DV), F32)

        def step(c, carry):
            keys = kb[2 * p : 2 * p + 2].reshape(2 * ROWS, 2 * DH)
            values = vb[2 * p : 2 * p + 2].reshape(2 * ROWS, DV)
            pair = pl.ds(2 * c, 2)
            queries = qb[pair].reshape(2 * ROWS, 2 * DH)
            grads = gb[pair, :ROWS].reshape(2 * ROWS, DV)
            numbers = stat[c]
            seen = kpos <= qpos[c, :1]
            key_one, key_two = keys[:, :DH], keys[:, DH:]
            query_one, query_two = queries[:, :DH], queries[:, DH:]
            far = ((1,), (1,))
            score_one = dot(key_one, query_one, far) * (scale * LOG2E) - numbers[0:1]
            score_two = dot(key_two, query_two, far) * (scale * LOG2E) - numbers[1:2]
            attn = dot(values, grads, far)
            prob_one = jnp.exp2(jnp.where(seen, score_one, -jnp.inf))
            prob_two = jnp.exp2(jnp.where(seen, score_two, -jnp.inf))
            grad_one = (prob_one * (attn - numbers[2:3])).astype(BF16)
            grad_two = (prob_two * (numbers[3:4] - attn)).astype(BF16)
            mix = (prob_one - prob_two).astype(BF16)
            near = ((1,), (0,))
            gk_sum[p, :, :DH] += dot(grad_one, query_one, near)
            gk_sum[p, :, DH:] += dot(grad_two, query_two, near)
            gv_sum[p] += dot(mix, grads, near)
            first = ((0,), (0,))
            gq_sum[pair, :, :DH] += dot(grad_one, key_one, first).reshape(2, ROWS, DH)
            gq_sum[pair, :, DH:] += dot(grad_two, key_two, first).reshape(2, ROWS, DH)
            return carry

        lax.fori_loop(0, 4, step, 0)

    total = {"k": gk_sum, "v": gv_sum}

    def mine(kind, d):
        slot = KSLOT[d % NZ]
        return total[kind][slot // 2, slot % 2 * ROWS : slot % 2 * ROWS + ROWS]

    spot = {"u": 0, "d": 1}

    def place(kind, way, d):
        return {"k": 0, "v": 1}[kind] + 2 * spot[way] + 4 * (d - 1)

    def pass_sum(kind, way, d, joined):
        value = mine(kind, -d if way == "u" else d)
        if joined:
            arrived(f"r{kind}{way}{d + 1}")
            value = value + zr[place(kind, way, d + 1)].astype(F32)
        i = place(kind, way, d)
        zs[i] = value.astype(BF16)
        go(f"r{kind}{way}{d}", zs.at[i], zr.at[i], up if way == "u" else down)

    tile(0)
    pass_sum("k", "u", 4, False)
    pass_sum("v", "d", 4, False)
    pass_sum("v", "u", 3, False)
    tile(1)
    pass_sum("k", "d", 3, False)
    pass_sum("k", "u", 3, True)
    pass_sum("v", "d", 3, True)
    tile(2)
    for way in "ud":
        for kind in "kv":
            pass_sum(kind, way, 2, True)
    tile(3)
    for dx in range(1, NX):
        xs[dx - 1] = gq_sum[qslot(dx, 1)].astype(BF16)
        go(f"s{dx}", xs.at[dx - 1], xr.at[dx - 1], x_peers[NX - dx])
    for dx in range(1, NX):
        xs[dx + 2] = gq_sum[qslot(dx, 0)].astype(BF16)
        go(f"t{dx}", xs.at[dx + 2], xr.at[dx + 2], x_peers[NX - dx])
    for way in "ud":
        for kind in "kv":
            pass_sum(kind, way, 1, True)
    value = gq_sum[qslot(0, 1)]
    for dx in range(1, NX):
        arrived(f"s{dx}")
        value = value + xr[dx - 1].astype(F32)
    ys[...] = value.astype(BF16)
    go("sy", ys, yr, across)
    value = gq_sum[qslot(0, 0)]
    for dx in range(1, NX):
        arrived(f"t{dx}")
        value = value + xr[dx + 2].astype(F32)
    gq_sum[qslot(0, 0)] = value
    for way in "ud":
        for kind in "kv":
            arrived(f"r{kind}{way}1")
    value = mine("k", 0) + zr[place("k", "u", 1)].astype(F32) + zr[place("k", "d", 1)].astype(F32)
    value = value * scale
    gk1[...] = value[:, :DH].astype(BF16)
    gk2[...] = value[:, DH:].astype(BF16)
    value = mine("v", 0) + zr[place("v", "u", 1)].astype(F32) + zr[place("v", "d", 1)].astype(F32)
    gv[...] = value.astype(BF16)
    arrived("sy")
    value = (gq_sum[qslot(0, 0)] + yr[...].astype(F32)) * scale
    gq1[...] = value[:, :DH].astype(BF16)
    gq2[...] = value[:, DH:].astype(BF16)
    for move in moves.values():
        move.wait_send()


def per_device(*arrays):
    q1, q2, k1, k2, v, o1, o2, totals, lam, gain, cot, block_of = arrays
    flat = lambda a: a.reshape(ROWS, a.shape[-1])
    vmem, smem = pl.BlockSpec(memory_space=pltpu.VMEM), pl.BlockSpec(memory_space=pltpu.SMEM)
    copies = 64
    shape = lambda width: jax.ShapeDtypeStruct((ROWS, width), BF16)
    out = pl.pallas_call(
        kernel,
        out_shape=[shape(DH)] * 4 + [shape(DV)],
        in_specs=[vmem] * 8 + [smem, vmem, vmem, smem],
        out_specs=[vmem] * 5,
        scratch_shapes=[
            pltpu.VMEM((NU, 16, DV), BF16),
            pltpu.VMEM((NU, 16, DV), BF16),
            pltpu.VMEM((8, ROWS, 2 * DH), BF16),
            pltpu.VMEM((8, GROWS, DV), BF16),
            pltpu.VMEM((8, ROWS, 2 * DH), BF16),
            pltpu.VMEM((8, ROWS, DV), BF16),
            pltpu.VMEM((4, 8, 2 * ROWS), F32),
            pltpu.VMEM((4, 8, 2 * ROWS), jnp.int32),
            pltpu.VMEM((8, ROWS, 2 * DH), F32),
            pltpu.VMEM((4, 2 * ROWS, 2 * DH), F32),
            pltpu.VMEM((4, 2 * ROWS, DV), F32),
            pltpu.VMEM((16, ROWS, DV), BF16),
            pltpu.VMEM((16, ROWS, DV), BF16),
            pltpu.VMEM((6, ROWS, 2 * DH), BF16),
            pltpu.VMEM((6, ROWS, 2 * DH), BF16),
            pltpu.VMEM((ROWS, 2 * DH), BF16),
            pltpu.VMEM((ROWS, 2 * DH), BF16),
            pltpu.SemaphoreType.DMA((copies,)),
            pltpu.SemaphoreType.DMA((copies,)),
        ],
        compiler_params=pltpu.CompilerParams(
            collective_id=0, has_side_effects=True, vmem_limit_bytes=48 * 1024 * 1024
        ),
    )(
        flat(q1), flat(q2), flat(k1), flat(k2), flat(v), flat(o1), flat(o2),
        totals, lam, gain, cot.reshape(16, NU, DV), block_of,
    )
    return tuple(g.reshape(2, HALF, 1, g.shape[-1]) for g in out)


def solution(mesh):
    rows = P("blk", None, "ulysses", None)
    in_specs = (rows,) * 7 + (
        P("ulysses", None, "blk", None),
        P("ulysses"),
        P("ulysses", None),
        P("blk", "ulysses", None, None),
        P(),
    )
    return jax.shard_map(
        per_device, mesh=mesh, in_specs=in_specs, out_specs=(rows,) * 5, check_vma=False
    )
```

```python
import functools
import math

import jax
import jax.numpy as jnp
from jax import lax
from jax.experimental import pallas as pl
from jax.experimental.pallas import tpu as pltpu
from jax.sharding import PartitionSpec as P

MESH = pl.DeviceIdType.MESH
NX, NZ, NY, NU = 4, 8, 2, 8
ROWS, DH, DV, HALF = 128, 128, 256, 64
GROWS = ROWS + 16
EPS = 1e-05
LOG2E = math.log2(math.e)
F32, BF16 = jnp.float32, jnp.bfloat16
KSLOT = {4: 0, 5: 1, 3: 2, 6: 3, 2: 4, 7: 5, 1: 6, 0: 7}
KFROM = {place: d for d, place in KSLOT.items()}


def qslot(dx, dy):
    return dx + (0 if dy else 4)


def dot(a, b, dims):
    return lax.dot_general(a, b, (dims, ((), ())), preferred_element_type=F32)


def split3(value):
    high = value.astype(BF16)
    rest = value - high.astype(F32)
    middle = rest.astype(BF16)
    low = (rest - middle.astype(F32)).astype(BF16)
    return high.astype(F32), middle.astype(F32), low.astype(F32)


def kernel(
    q1, q2, k1, k2, v, o1_in, o2_in, totals_in, lam_ref, gain_in, cot_in_hbm, block_of,
    grads_out,
    o1, o2, totals, gain, cot, local, cot_out, cot_in, qb, gb, kb, vb, stat, qpos, kpos, gq_sum, gk_sum, gv_sum,
    zs, zr, xs, xr, ys, yr, send, recv,
):
    u = lax.axis_index("ulysses")
    blk = lax.axis_index("blk")
    x, z, y = blk // (NZ * NY), (blk // NY) % NZ, blk % NY

    def at(nx, nz, ny):
        return {"blk": (lax.rem(nx, NX) * NZ + lax.rem(nz, NZ)) * NY + lax.rem(ny, NY)}

    up, down, across = at(x, z + 1, y), at(x, z + NZ - 1, y), at(x, z, y + 1)
    x_peers = {dx: at(x + dx, z, y) for dx in range(1, NX)}
    u_peers = {r: {"ulysses": lax.rem(u + r, NU)} for r in range(1, NU)}

    moves = {}

    def view(place):
        return place[0].at[place[1:]] if isinstance(place, tuple) else place

    def move(name):
        i, src, dst, device = moves[name]
        return pltpu.make_async_remote_copy(
            src_ref=view(src), dst_ref=view(dst), send_sem=send.at[i], recv_sem=recv.at[i],
            device_id=device, device_id_type=MESH,
        )

    def go(name, src, dst, device):
        moves[name] = (len(moves), src, dst, device)
        move(name).start()

    def arrived(name):
        move(name).wait_recv()

    own_q, own_k = qslot(0, 0), KSLOT[0]
    loads = []
    for i, (src, dst) in enumerate((
        (cot_in_hbm, cot),
        (k1, kb.at[own_k, :, :DH]), (k2, kb.at[own_k, :, DH:]), (v, vb.at[own_k]),
        (q1, qb.at[own_q, :, :DH]), (q2, qb.at[own_q, :, DH:]),
        (o1_in, o1), (o2_in, o2), (totals_in, totals), (gain_in, gain),
    )):
        load = pltpu.make_async_copy(src, dst, local.at[i])
        load.start()
        loads.append(load)
    first_load, *loads = loads
    barrier = pltpu.get_barrier_semaphore()
    partners = [up, down, across, *x_peers.values(), *u_peers.values()]
    for partner in partners:
        pl.semaphore_signal(barrier, inc=1, device_id=partner, device_id_type=MESH)

    first_load.wait()
    to_row = lax.broadcasted_iota(jnp.int32, (ROWS, ROWS), 0)
    from_row = lax.broadcasted_iota(jnp.int32, (ROWS, ROWS), 1)
    wanted = (to_row % 16) * 8 + to_row // 16
    order = jnp.where(from_row == wanted, 1.0, 0.0).astype(BF16)
    rows_in = cot[...].astype(F32).reshape(ROWS, DV).astype(BF16)
    by_head = dot(order, rows_in, ((1,), (0,))).astype(BF16).reshape(NU, 16, DV)
    cot_out[...] = by_head

    for load in loads:
        load.wait()
    pl.semaphore_wait(barrier, len(partners))

    for r, device in u_peers.items():
        go(f"c{r}", (cot_out, lax.rem(u + r, NU)), (cot_in, u), device)
    for way, device, sign in (("u", up, 1), ("d", down, -1)):
        slot = KSLOT[sign % NZ]
        go(f"k{way}1", (kb, own_k), (kb, slot), device)
        go(f"v{way}1", (vb, own_k), (vb, slot), device)
    go("qy", (qb, own_q), (qb, qslot(0, 1)), across)
    for dx, device in x_peers.items():
        go(f"q{dx}", (qb, own_q), (qb, qslot(dx, 0)), device)

    cot_in[u] = cot_out[u]
    for r in u_peers:
        arrived(f"c{r}")
    lam = lam_ref[0]
    parts = cot_in[...].astype(F32)
    grad_y = jnp.concatenate(
        [parts[w, s * 8 : s * 8 + 8] for s in range(2) for w in range(NU)], axis=0
    )
    first_out, second_out = o1[...].astype(F32), o2[...].astype(F32)
    combined = first_out - lam * second_out
    inv_rms = lax.rsqrt(jnp.mean(combined * combined, axis=-1, keepdims=True) + EPS)
    gained = gain[...] * grad_y
    centre = jnp.mean(combined * gained, axis=-1, keepdims=True)
    grad_out = (inv_rms * (gained - combined * inv_rms * inv_rms * centre)).astype(BF16)
    gb[own_q, :ROWS] = grad_out
    wide = grad_out.astype(F32)
    dot_one = jnp.sum(wide * first_out, axis=-1, keepdims=True)
    dot_two = jnp.sum(wide * second_out, axis=-1, keepdims=True)
    row_one = jnp.broadcast_to(dot_one, (ROWS, ROWS)).T[:1]
    row_two = jnp.broadcast_to(dot_two, (ROWS, ROWS)).T[:1]
    log_lam = jnp.log2(jnp.full((1, ROWS), lam, F32))
    total_one = jnp.concatenate([totals[0, 0, :1], totals[0, 0, 1:]], axis=1) * LOG2E
    total_two = jnp.concatenate([totals[0, 1, :1], totals[0, 1, 1:]], axis=1) * LOG2E
    stats = jnp.concatenate([total_one, total_two - log_lam, row_one, row_two], axis=0)
    coded = jnp.concatenate([*split3(stats), jnp.zeros((4, ROWS), F32)], axis=0)
    gb[own_q, ROWS:] = jnp.concatenate([coded, jnp.zeros((16, ROWS), F32)], axis=1).astype(BF16)

    go("gy", (gb, own_q), (gb, qslot(0, 1)), across)
    for dx, device in x_peers.items():
        go(f"g{dx}", (gb, own_q), (gb, qslot(dx, 0)), device)

    def pass_on(hop, kinds):
        for kind, way, device, sign in kinds:
            arrived(f"{kind}{way}{hop}")
            held = {"k": kb, "v": vb}[kind]
            here, there = KSLOT[sign * hop % NZ], KSLOT[sign * (hop + 1) % NZ]
            go(f"{kind}{way}{hop + 1}", (held, here), (held, there), device)

    both = [(kind, way, device, sign) for way, device, sign in (("u", up, 1), ("d", down, -1)) for kind in "kv"]
    pass_on(1, both)
    arrived("qy")
    for dx, device in x_peers.items():
        go(f"p{dx}", (qb, qslot(0, 1)), (qb, qslot(dx, 1)), device)

    lane = lax.broadcasted_iota(jnp.int32, (8, 4 * HALF), 1)
    for dy in range(NY):
        sources = [at(x + NX - dx, z, y + dy)["blk"] for dx in range(NX)]
        for half in range(2):
            starts = [block_of[2 * source + half] for source in sources]
            start = jnp.where(
                lane < 2 * HALF,
                jnp.where(lane < HALF, starts[0], starts[1]),
                jnp.where(lane < 3 * HALF, starts[2], starts[3]),
            )
            qpos[dy, half] = start * HALF + lane % HALF
    row = lax.broadcasted_iota(jnp.int32, (ROWS, ROWS), 0)
    for slot in range(NZ):
        source = at(x, z + NZ - KFROM[slot], y)["blk"]
        low, high = block_of[2 * source], block_of[2 * source + 1]
        kpos[slot] = jnp.where(row < HALF, low * HALF + row, high * HALF + row - HALF)
    gq_sum[...] = jnp.zeros_like(gq_sum)
    gk_sum[...] = jnp.zeros_like(gk_sum)
    gv_sum[...] = jnp.zeros_like(gv_sum)
    scale = 1.0 / math.sqrt(DH)

    def unpack_stats(dy):
        whole = []
        for dx in range(NX):
            coded = gb[qslot(dx, dy), ROWS:, :ROWS].astype(F32)
            whole.append(coded[0:4] + coded[4:8] + coded[8:12])
        for half in range(2):
            part = slice(half * HALF, half * HALF + HALF)
            for side in range(2):
                pair = [w[:, part] for w in whole[2 * side : 2 * side + 2]]
                stat[dy, half, 0:4, side * ROWS : side * ROWS + ROWS] = jnp.concatenate(pair, axis=1)

    far, near, first = ((1,), (1,)), ((1,), (0,)), ((0,), (0,))

    def scores(keys, values, queries, grads):
        return (
            dot(keys[:, :DH], queries[:, :DH], far),
            dot(keys[:, DH:], queries[:, DH:], far),
            dot(values, grads, far),
        )

    def weights(raw, numbers, places, query_places):
        one, two, attn = raw
        seen = jnp.concatenate([places, places], axis=1) <= query_places
        one = one * (scale * LOG2E) - numbers[0:1]
        two = two * (scale * LOG2E) - numbers[1:2]
        prob_one = jnp.exp2(jnp.where(seen, one, -jnp.inf))
        prob_two = jnp.exp2(jnp.where(seen, two, -jnp.inf))
        grad_one = (prob_one * (attn - numbers[2:3])).astype(BF16)
        grad_two = (prob_two * (numbers[3:4] - attn)).astype(BF16)
        return grad_one, grad_two, (prob_one - prob_two).astype(BF16)

    def tile(i):
        early = i < 4
        dy = jnp.where(early, 0, 1)
        pair = pl.ds(2 * jnp.where(early, 3 - i, i - 4), 2)
        four = pl.ds(jnp.where(early, 4, 0), 4)
        keys = kb[pair].reshape(2 * ROWS, 2 * DH)
        values = vb[pair].reshape(2 * ROWS, DV)
        low_keys = kb[pair, :HALF].reshape(ROWS, 2 * DH)
        low_values = vb[pair, :HALF].reshape(ROWS, DV)
        queries = qb[four, HALF:].reshape(4 * HALF, 2 * DH)
        grads = gb[four, HALF:ROWS].reshape(4 * HALF, DV)
        low_queries = qb[four, :HALF].reshape(4 * HALF, 2 * DH)
        low_grads = gb[four, :HALF].reshape(4 * HALF, DV)
        high_raw = scores(keys, values, queries, grads)
        low_raw = scores(low_keys, low_values, low_queries, low_grads)
        one, two, mix = weights(high_raw, stat[dy, 1], kpos[pair].reshape(2 * ROWS, ROWS), qpos[dy, 1, :1])
        low_one, low_two, low_mix = weights(
            low_raw, stat[dy, 0], kpos[pair, :HALF].reshape(ROWS, ROWS), qpos[dy, 0, :1]
        )
        gq_sum[four, HALF:, :DH] += dot(one, keys[:, :DH], first).reshape(4, HALF, DH)
        gq_sum[four, HALF:, DH:] += dot(two, keys[:, DH:], first).reshape(4, HALF, DH)
        nothing = jnp.zeros((ROWS, DH), BF16)
        apart = jnp.concatenate(
            [
                jnp.concatenate([low_keys[:, :DH], nothing], axis=1),
                jnp.concatenate([nothing, low_keys[:, DH:]], axis=1),
            ],
            axis=0,
        )
        stacked = jnp.concatenate([low_one, low_two], axis=0)
        gq_sum[four, :HALF] += dot(stacked, apart, first).reshape(4, HALF, 2 * DH)
        gk_sum[pair, :, :DH] += dot(one, queries[:, :DH], near).reshape(2, ROWS, DH)
        gk_sum[pair, :, DH:] += dot(two, queries[:, DH:], near).reshape(2, ROWS, DH)
        gv_sum[pair] += dot(mix, grads, near).reshape(2, ROWS, DV)
        gk_sum[pair, :HALF, :DH] += dot(low_one, low_queries[:, :DH], near).reshape(2, HALF, DH)
        gk_sum[pair, :HALF, DH:] += dot(low_two, low_queries[:, DH:], near).reshape(2, HALF, DH)
        gv_sum[pair, :HALF] += dot(low_mix, low_grads, near).reshape(2, HALF, DV)

    total = {"k": gk_sum, "v": gv_sum}

    def mine(kind, d):
        return total[kind][KSLOT[d % NZ]]

    spot = {"u": 0, "d": 1}

    def place(kind, way, d):
        return {"k": 0, "v": 1}[kind] + 2 * spot[way] + 4 * (d - 1)

    def pass_sum(kind, way, d, joined):
        value = mine(kind, -d if way == "u" else d)
        if joined:
            arrived(f"r{kind}{way}{d + 1}")
            value = value + zr[place(kind, way, d + 1)].astype(F32)
        i = place(kind, way, d)
        zs[i] = value.astype(BF16)
        go(f"r{kind}{way}{d}", (zs, i), (zr, i), up if way == "u" else down)

    def send_queries(dy, sends, first_at):
        for dx in range(1, NX):
            xs[dx + first_at] = gq_sum[qslot(dx, dy)].astype(BF16)
            go(f"{sends}{dx}", (xs, dx + first_at), (xr, dx + first_at), x_peers[NX - dx])

    def step(i, carry):
        @pl.when(i == 0)
        def _():
            for dx in x_peers:
                arrived(f"q{dx}")
                arrived(f"g{dx}")
            unpack_stats(0)

        @pl.when(i == 1)
        def _():
            pass_on(2, both)

        @pl.when(i == 2)
        def _():
            arrived("gy")
            for dx, device in x_peers.items():
                go(f"h{dx}", (gb, qslot(0, 1)), (gb, qslot(dx, 1)), device)
            pass_on(3, [both[0], both[3]])
            arrived("vu3")
            arrived("kd3")

        @pl.when(i == 3)
        def _():
            arrived("ku4")
            arrived("vd4")

        @pl.when(i == 4)
        def _():
            send_queries(0, "t", 2)
            for dx in x_peers:
                arrived(f"p{dx}")
                arrived(f"h{dx}")
            unpack_stats(1)

        @pl.when(i == 5)
        def _():
            pass_sum("k", "u", 4, False)
            pass_sum("v", "d", 4, False)
            pass_sum("v", "u", 3, False)

        @pl.when(i == 6)
        def _():
            pass_sum("k", "d", 3, False)

        tile(i)
        return carry

    lax.fori_loop(0, 8, step, 0)
    send_queries(1, "s", -1)
    pass_sum("k", "u", 3, True)
    pass_sum("v", "d", 3, True)
    pass_sum("v", "u", 2, True)
    pass_sum("k", "d", 2, True)
    pass_sum("k", "u", 2, True)
    pass_sum("v", "d", 2, True)
    value = gq_sum[qslot(0, 1)]
    for dx in range(1, NX):
        arrived(f"s{dx}")
        value = value + xr[dx - 1].astype(F32)
    ys[...] = value.astype(BF16)
    go("sy", ys, yr, across)
    pass_sum("v", "u", 1, True)
    pass_sum("k", "d", 1, True)
    pass_sum("k", "u", 1, True)
    pass_sum("v", "d", 1, True)
    value = gq_sum[qslot(0, 0)]
    for dx in range(1, NX):
        arrived(f"t{dx}")
        value = value + xr[dx + 2].astype(F32)
    gq_sum[qslot(0, 0)] = value
    for way in "ud":
        for kind in "kv":
            arrived(f"r{kind}{way}1")
    value = mine("k", 0) + zr[place("k", "u", 1)].astype(F32) + zr[place("k", "d", 1)].astype(F32)
    value = value * scale
    grads_out[1] = value.astype(BF16)
    value = mine("v", 0) + zr[place("v", "u", 1)].astype(F32) + zr[place("v", "d", 1)].astype(F32)
    grads_out[2] = value.astype(BF16)
    arrived("sy")
    value = (gq_sum[qslot(0, 0)] + yr[...].astype(F32)) * scale
    grads_out[0] = value.astype(BF16)
    for name in moves:
        move(name).wait_send()


def finish(grads, gq1, gq2, gk1, gk2, gv, done):
    moves = [
        pltpu.make_async_copy(src, dst, done.at[i])
        for i, (src, dst) in enumerate((
            (grads.at[0, :, :DH], gq1), (grads.at[0, :, DH:], gq2),
            (grads.at[1, :, :DH], gk1), (grads.at[1, :, DH:], gk2), (grads.at[2], gv),
        ))
    ]
    for move in moves:
        move.start()
    for move in moves:
        move.wait()


def per_device(*arrays):
    q1, q2, k1, k2, v, o1, o2, totals, lam, gain, cot, block_of = arrays
    flat = lambda a: a.reshape(ROWS, a.shape[-1])
    hbm = pl.BlockSpec(memory_space=pltpu.HBM)
    vmem, smem = pl.BlockSpec(memory_space=pltpu.VMEM), pl.BlockSpec(memory_space=pltpu.SMEM)
    copies = 64
    shape = lambda width: jax.ShapeDtypeStruct((ROWS, width), BF16)
    grads = pl.pallas_call(
        kernel,
        out_shape=jax.ShapeDtypeStruct((3, ROWS, DV), BF16),
        in_specs=[hbm] * 8 + [smem, hbm, hbm, smem],
        out_specs=vmem,
        scratch_shapes=[
            pltpu.VMEM((ROWS, DV), BF16),
            pltpu.VMEM((ROWS, DV), BF16),
            pltpu.VMEM((1, 2, 2, HALF), F32),
            pltpu.VMEM((1, DV), F32),
            pltpu.VMEM((16, NU, DV), BF16),
            pltpu.SemaphoreType.DMA((10,)),
            pltpu.VMEM((NU, 16, DV), BF16),
            pltpu.VMEM((NU, 16, DV), BF16),
            pltpu.VMEM((8, ROWS, 2 * DH), BF16),
            pltpu.VMEM((8, GROWS, DV), BF16),
            pltpu.VMEM((8, ROWS, 2 * DH), BF16),
            pltpu.VMEM((8, ROWS, DV), BF16),
            pltpu.VMEM((2, 2, 8, 4 * HALF), F32),
            pltpu.VMEM((2, 2, 8, 4 * HALF), jnp.int32),
            pltpu.VMEM((8, ROWS, ROWS), jnp.int32),
            pltpu.VMEM((8, ROWS, 2 * DH), F32),
            pltpu.VMEM((8, ROWS, 2 * DH), F32),
            pltpu.VMEM((8, ROWS, DV), F32),
            pltpu.VMEM((16, ROWS, DV), BF16),
            pltpu.VMEM((16, ROWS, DV), BF16),
            pltpu.VMEM((6, ROWS, 2 * DH), BF16),
            pltpu.VMEM((6, ROWS, 2 * DH), BF16),
            pltpu.VMEM((ROWS, 2 * DH), BF16),
            pltpu.VMEM((ROWS, 2 * DH), BF16),
            pltpu.SemaphoreType.DMA((copies,)),
            pltpu.SemaphoreType.DMA((copies,)),
        ],
        compiler_params=pltpu.CompilerParams(
            collective_id=0, has_side_effects=True, vmem_limit_bytes=56 * 1024 * 1024
        ),
    )(
        flat(q1), flat(q2), flat(k1), flat(k2), flat(v), flat(o1), flat(o2),
        totals, lam, gain, cot.reshape(16, NU, DV), block_of,
    )
    out = pl.pallas_call(
        finish,
        out_shape=[shape(DH)] * 4 + [shape(DV)],
        in_specs=[vmem],
        out_specs=[hbm] * 5,
        scratch_shapes=[pltpu.SemaphoreType.DMA((5,))],
    )(grads)
    return tuple(g.reshape(2, HALF, 1, g.shape[-1]) for g in out)


def solution(mesh):
    rows = P("blk", None, "ulysses", None)
    in_specs = (rows,) * 7 + (
        P("ulysses", None, "blk", None),
        P("ulysses"),
        P("ulysses", None),
        P("blk", "ulysses", None, None),
        P(),
    )
    return jax.shard_map(
        per_device, mesh=mesh, in_specs=in_specs, out_specs=(rows,) * 5, check_vma=False
    )
```

```python
import functools
import math

import jax
import jax.numpy as jnp
from jax import lax
from jax.experimental import pallas as pl
from jax.experimental.pallas import tpu as pltpu
from jax.sharding import PartitionSpec as P

MESH = pl.DeviceIdType.MESH
NX, NZ, NY, NU = 4, 8, 2, 8
ROWS, DH, DV, HALF = 128, 128, 256, 64
GROWS = ROWS + 16
EPS = 1e-05
LOG2E = math.log2(math.e)
F32, BF16 = jnp.float32, jnp.bfloat16
PARTS = (slice(0, HALF), slice(HALF, ROWS))
G_PARTS = (slice(0, HALF), slice(HALF, GROWS))
KSLOT = {4: 0, 5: 1, 3: 2, 6: 3, 2: 4, 7: 5, 1: 6, 0: 7}
KFROM = {place: d for d, place in KSLOT.items()}


def qslot(dx, dy):
    return dx + (0 if dy else 4)


def dot(a, b, dims):
    return lax.dot_general(a, b, (dims, ((), ())), preferred_element_type=F32)


def split3(value):
    high = value.astype(BF16)
    rest = value - high.astype(F32)
    middle = rest.astype(BF16)
    low = (rest - middle.astype(F32)).astype(BF16)
    return high.astype(F32), middle.astype(F32), low.astype(F32)


def kernel(
    q1, q2, k1, k2, v, o1_in, o2_in, totals_in, lam_ref, gain_in, cot_in_hbm, block_in,
    grads_out,
    o1, o2, totals, gain, cot, block_of, local, cot_out, cot_in, qb, gb, kb, vb, stat, qpos, kpos, gq_sum, gk_sum, gv_sum,
    zs, zr, xs, xr, ys, yr, send, recv,
):
    u = lax.axis_index("ulysses")
    blk = lax.axis_index("blk")
    x, z, y = blk // (NZ * NY), (blk // NY) % NZ, blk % NY

    def at(nx, nz, ny):
        return {"blk": (lax.rem(nx, NX) * NZ + lax.rem(nz, NZ)) * NY + lax.rem(ny, NY)}

    up, down, across = at(x, z + 1, y), at(x, z + NZ - 1, y), at(x, z, y + 1)
    x_peers = {dx: at(x + dx, z, y) for dx in (2, 1, 3)}
    u_peers = {r: {"ulysses": lax.rem(u + r, NU)} for r in range(1, NU)}

    moves = {}

    def view(place):
        return place[0].at[place[1:]] if isinstance(place, tuple) else place

    def move(name):
        i, src, dst, device = moves[name]
        return pltpu.make_async_remote_copy(
            src_ref=view(src), dst_ref=view(dst), send_sem=send.at[i], recv_sem=recv.at[i],
            device_id=device, device_id_type=MESH,
        )

    def go(name, src, dst, device):
        moves[name] = (len(moves), src, dst, device)
        move(name).start()

    def arrived(name):
        move(name).wait_recv()

    own_q, own_k = qslot(0, 0), KSLOT[0]
    loads = []
    for i, (src, dst) in enumerate((
        (cot_in_hbm, cot),
        (k1, kb.at[own_k, :, :DH]), (k2, kb.at[own_k, :, DH:]), (v, vb.at[own_k]),
        (q1, qb.at[own_q, :, :DH]), (q2, qb.at[own_q, :, DH:]),
        (o1_in, o1), (o2_in, o2), (totals_in, totals), (gain_in, gain),
            (block_in, block_of),
    )):
        load = pltpu.make_async_copy(src, dst, local.at[i])
        load.start()
        loads.append(load)
    first_load, *loads = loads
    barrier = pltpu.get_barrier_semaphore()
    partners = [up, down, across, *x_peers.values(), *u_peers.values()]
    for partner in partners:
        pl.semaphore_signal(barrier, inc=1, device_id=partner, device_id_type=MESH)

    first_load.wait()
    to_row = lax.broadcasted_iota(jnp.int32, (ROWS, ROWS), 0)
    from_row = lax.broadcasted_iota(jnp.int32, (ROWS, ROWS), 1)
    wanted = (to_row % 16) * 8 + to_row // 16
    order = jnp.where(from_row == wanted, 1.0, 0.0).astype(BF16)
    rows_in = cot[...].astype(F32).reshape(ROWS, DV).astype(BF16)
    by_head = dot(order, rows_in, ((1,), (0,))).astype(BF16).reshape(NU, 16, DV)
    cot_out[...] = by_head

    for load in loads:
        load.wait()
    lane = lax.broadcasted_iota(jnp.int32, (8, 4 * HALF), 1)
    for dy in range(NY):
        sources = [at(x + NX - dx, z, y + dy)["blk"] for dx in range(NX)]
        for half in range(2):
            starts = [block_of[2 * source + half] for source in sources]
            start = jnp.where(
                lane < 2 * HALF,
                jnp.where(lane < HALF, starts[0], starts[1]),
                jnp.where(lane < 3 * HALF, starts[2], starts[3]),
            )
            qpos[dy, half] = start * HALF + lane % HALF
    row = lax.broadcasted_iota(jnp.int32, (ROWS, ROWS), 0)
    for slot in range(NZ):
        source = at(x, z + NZ - KFROM[slot], y)["blk"]
        low, high = block_of[2 * source], block_of[2 * source + 1]
        kpos[slot] = jnp.where(row < HALF, low * HALF + row, high * HALF + row - HALF)
    gq_sum[...] = jnp.zeros_like(gq_sum)
    gk_sum[...] = jnp.zeros_like(gk_sum)
    gv_sum[...] = jnp.zeros_like(gv_sum)
    pl.semaphore_wait(barrier, len(partners))

    for r, device in u_peers.items():
        go(f"c{r}", (cot_out, lax.rem(u + r, NU)), (cot_in, u), device)
    for way, device, sign in (("u", up, 1), ("d", down, -1)):
        slot = KSLOT[sign % NZ]
        go(f"k{way}1", (kb, own_k), (kb, slot), device)
    for way, device, sign in (("u", up, 1), ("d", down, -1)):
        slot = KSLOT[sign % NZ]
        go(f"v{way}1", (vb, own_k), (vb, slot), device)
    go("qy", (qb, own_q), (qb, qslot(0, 1)), across)
    for dx, device in x_peers.items():
        go(f"q{dx}", (qb, own_q), (qb, qslot(dx, 0)), device)

    def pass_on(hop, kinds):
        for kind, way, device, sign in kinds:
            arrived(f"{kind}{way}{hop}")
            held = {"k": kb, "v": vb}[kind]
            here, there = KSLOT[sign * hop % NZ], KSLOT[sign * (hop + 1) % NZ]
            go(f"{kind}{way}{hop + 1}", (held, here), (held, there), device)

    both = [(kind, way, device, sign) for kind in "kv" for way, device, sign in (("u", up, 1), ("d", down, -1))]
    cot_in[u] = cot_out[u]
    pass_on(1, both)
    for r in u_peers:
        arrived(f"c{r}")
    lam = lam_ref[0]
    parts = cot_in[...].astype(F32)
    grad_y = jnp.concatenate(
        [parts[w, s * 8 : s * 8 + 8] for s in range(2) for w in range(NU)], axis=0
    )
    first_out, second_out = o1[...].astype(F32), o2[...].astype(F32)
    combined = first_out - lam * second_out
    inv_rms = lax.rsqrt(jnp.mean(combined * combined, axis=-1, keepdims=True) + EPS)
    gained = gain[...] * grad_y
    centre = jnp.mean(combined * gained, axis=-1, keepdims=True)
    grad_out = (inv_rms * (gained - combined * inv_rms * inv_rms * centre)).astype(BF16)
    gb[own_q, :ROWS] = grad_out
    wide = grad_out.astype(F32)
    dot_one = jnp.sum(wide * first_out, axis=-1, keepdims=True)
    dot_two = jnp.sum(wide * second_out, axis=-1, keepdims=True)
    row_one = jnp.broadcast_to(dot_one, (ROWS, ROWS)).T[:1]
    row_two = jnp.broadcast_to(dot_two, (ROWS, ROWS)).T[:1]
    log_lam = jnp.log2(jnp.full((1, ROWS), lam, F32))
    total_one = jnp.concatenate([totals[0, 0, :1], totals[0, 0, 1:]], axis=1) * LOG2E
    total_two = jnp.concatenate([totals[0, 1, :1], totals[0, 1, 1:]], axis=1) * LOG2E
    stats = jnp.concatenate([total_one, total_two - log_lam, row_one, row_two], axis=0)
    coded = jnp.concatenate([*split3(stats), jnp.zeros((4, ROWS), F32)], axis=0)
    gb[own_q, ROWS:] = jnp.concatenate([coded, jnp.zeros((16, ROWS), F32)], axis=1).astype(BF16)

    for part, rows in enumerate(G_PARTS):
        go(f"gy{part}", (gb, own_q, rows), (gb, qslot(0, 1), rows), across)
    for dx, device in x_peers.items():
        go(f"g{dx}", (gb, own_q), (gb, qslot(dx, 0)), device)

    pass_on(2, both[:2])
    arrived("qy")
    for dx, device in x_peers.items():
        go(f"p{dx}", (qb, qslot(0, 1)), (qb, qslot(dx, 1)), device)
    pass_on(2, both[2:])

    scale = 1.0 / math.sqrt(DH)

    def unpack_stats(dy):
        whole = []
        for dx in range(NX):
            coded = gb[qslot(dx, dy), ROWS:, :ROWS].astype(F32)
            whole.append(coded[0:4] + coded[4:8] + coded[8:12])
        for half in range(2):
            part = slice(half * HALF, half * HALF + HALF)
            for side in range(2):
                pair = [w[:, part] for w in whole[2 * side : 2 * side + 2]]
                stat[dy, half, 0:4, side * ROWS : side * ROWS + ROWS] = jnp.concatenate(pair, axis=1)

    far, near, first = ((1,), (1,)), ((1,), (0,)), ((0,), (0,))

    def scores(keys, values, queries, grads):
        return (
            dot(keys[:, :DH], queries[:, :DH], far),
            dot(keys[:, DH:], queries[:, DH:], far),
            dot(values, grads, far),
        )

    def weights(raw, numbers, places, query_places):
        one, two, attn = raw
        seen = jnp.concatenate([places, places], axis=1) <= query_places
        one = one * (scale * LOG2E) - numbers[0:1]
        two = two * (scale * LOG2E) - numbers[1:2]
        prob_one = jnp.exp2(jnp.where(seen, one, -jnp.inf))
        prob_two = jnp.exp2(jnp.where(seen, two, -jnp.inf))
        grad_one = (prob_one * (attn - numbers[2:3])).astype(BF16)
        grad_two = (prob_two * (numbers[3:4] - attn)).astype(BF16)
        return grad_one, grad_two, (prob_one - prob_two).astype(BF16)

    def tile(i):
        early = i < 4
        dy = jnp.where(early, 0, 1)
        pair = pl.ds(2 * jnp.where(early, 3 - i, i - 4), 2)
        four = pl.ds(jnp.where(early, 4, 0), 4)
        keys = kb[pair].reshape(2 * ROWS, 2 * DH)
        values = vb[pair].reshape(2 * ROWS, DV)
        low_keys = kb[pair, :HALF].reshape(ROWS, 2 * DH)
        low_values = vb[pair, :HALF].reshape(ROWS, DV)
        queries = qb[four, HALF:].reshape(4 * HALF, 2 * DH)
        grads = gb[four, HALF:ROWS].reshape(4 * HALF, DV)
        low_queries = qb[four, :HALF].reshape(4 * HALF, 2 * DH)
        low_grads = gb[four, :HALF].reshape(4 * HALF, DV)
        high_raw = scores(keys, values, queries, grads)
        low_raw = scores(low_keys, low_values, low_queries, low_grads)
        one, two, mix = weights(high_raw, stat[dy, 1], kpos[pair].reshape(2 * ROWS, ROWS), qpos[dy, 1, :1])
        low_one, low_two, low_mix = weights(
            low_raw, stat[dy, 0], kpos[pair, :HALF].reshape(ROWS, ROWS), qpos[dy, 0, :1]
        )
        gq_sum[four, HALF:, :DH] += dot(one, keys[:, :DH], first).reshape(4, HALF, DH)
        gq_sum[four, HALF:, DH:] += dot(two, keys[:, DH:], first).reshape(4, HALF, DH)
        nothing = jnp.zeros((ROWS, DH), BF16)
        apart = jnp.concatenate(
            [
                jnp.concatenate([low_keys[:, :DH], nothing], axis=1),
                jnp.concatenate([nothing, low_keys[:, DH:]], axis=1),
            ],
            axis=0,
        )
        stacked = jnp.concatenate([low_one, low_two], axis=0)
        gq_sum[four, :HALF] += dot(stacked, apart, first).reshape(4, HALF, 2 * DH)
        gk_sum[pair, :, :DH] += dot(one, queries[:, :DH], near).reshape(2, ROWS, DH)
        gk_sum[pair, :, DH:] += dot(two, queries[:, DH:], near).reshape(2, ROWS, DH)
        gv_sum[pair] += dot(mix, grads, near).reshape(2, ROWS, DV)
        gk_sum[pair, :HALF, :DH] += dot(low_one, low_queries[:, :DH], near).reshape(2, HALF, DH)
        gk_sum[pair, :HALF, DH:] += dot(low_two, low_queries[:, DH:], near).reshape(2, HALF, DH)
        gv_sum[pair, :HALF] += dot(low_mix, low_grads, near).reshape(2, HALF, DV)

    total = {"k": gk_sum, "v": gv_sum}

    spot = {"u": 0, "d": 1}

    def place(kind, way, d):
        return {"k": 0, "v": 1}[kind] + 2 * spot[way] + 4 * (d - 1)

    def pass_sum(kind, way, d, joined, part):
        rows = PARTS[part]
        value = total[kind][KSLOT[(-d if way == "u" else d) % NZ], rows]
        if joined:
            arrived(f"r{kind}{way}{d + 1}{part}")
            value = value + zr[place(kind, way, d + 1), rows].astype(F32)
        i = place(kind, way, d)
        zs[i, rows] = value.astype(BF16)
        go(f"r{kind}{way}{d}{part}", (zs, i, rows), (zr, i, rows), up if way == "u" else down)

    def pass_sums(kinds, d, joined):
        for part in range(len(PARTS)):
            for kind, way in zip(kinds, "ud"):
                if kind in "kv":
                    pass_sum(kind, way, d, joined, part)

    def send_queries(dy, sends, first_at):
        for part, rows in enumerate(PARTS):
            for dx in (2, 1, 3):
                i = dx + first_at
                xs[i, rows] = gq_sum[qslot(dx, dy), rows].astype(BF16)
                go(f"{sends}{dx}{part}", (xs, i, rows), (xr, i, rows), x_peers[NX - dx])

    def step(i, carry):
        @pl.when(i == 0)
        def _():
            pass_on(3, both[:1])
            for dx in x_peers:
                arrived(f"q{dx}")
                arrived(f"g{dx}")
            unpack_stats(0)
            pass_on(3, both[3:])

        @pl.when(i == 1)
        def _():
            for part, rows in enumerate(G_PARTS):
                arrived(f"gy{part}")
                for dx, device in x_peers.items():
                    go(f"h{dx}{part}", (gb, qslot(0, 1), rows), (gb, qslot(dx, 1), rows), device)

        @pl.when(i == 2)
        def _():
            arrived("vu3")
            arrived("kd3")

        @pl.when(i == 3)
        def _():
            arrived("ku4")
            arrived("vd4")

        @pl.when(i == 4)
        def _():
            send_queries(0, "t", 2)
            for dx in x_peers:
                arrived(f"p{dx}")
                for part in range(len(G_PARTS)):
                    arrived(f"h{dx}{part}")
            unpack_stats(1)

        @pl.when(i == 5)
        def _():
            pass_sums("kv", 4, False)
            pass_sums("v-", 3, False)

        @pl.when(i == 6)
        def _():
            pass_sums("-k", 3, False)

        tile(i)
        return carry

    lax.fori_loop(0, 8, step, 0)
    send_queries(1, "s", -1)
    pass_sums("kv", 3, True)
    pass_sums("vk", 2, True)
    for part, rows in enumerate(PARTS):
        value = gq_sum[qslot(0, 1), rows]
        for dx in (1, 3, 2):
            arrived(f"s{dx}{part}")
            value = value + xr[dx - 1, rows].astype(F32)
        ys[rows] = value.astype(BF16)
        go(f"sy{part}", (ys, rows), (yr, rows), across)
    pass_sums("kv", 2, True)
    pass_sums("vk", 1, True)
    for part, rows in enumerate(PARTS):
        value = gq_sum[qslot(0, 0), rows]
        for dx in range(1, NX):
            arrived(f"t{dx}{part}")
            value = value + xr[dx + 2, rows].astype(F32)
        gq_sum[qslot(0, 0), rows] = value
    pass_sums("kv", 1, True)
    for part, rows in enumerate(PARTS):
        for kind in "vk":
            value = total[kind][KSLOT[0], rows]
            for way in "ud":
                arrived(f"r{kind}{way}1{part}")
                value = value + zr[place(kind, way, 1), rows].astype(F32)
            if kind == "k":
                grads_out[1, rows] = (value * scale).astype(BF16)
            else:
                grads_out[2, rows] = value.astype(BF16)
    for part, rows in enumerate(PARTS):
        arrived(f"sy{part}")
        value = (gq_sum[qslot(0, 0), rows] + yr[rows].astype(F32)) * scale
        grads_out[0, rows] = value.astype(BF16)
    for name in moves:
        move(name).wait_send()


def finish(grads, gq1, gq2, gk1, gk2, gv, done):
    moves = [
        pltpu.make_async_copy(src, dst, done.at[i])
        for i, (src, dst) in enumerate((
            (grads.at[0, :, :DH], gq1), (grads.at[0, :, DH:], gq2),
            (grads.at[1, :, :DH], gk1), (grads.at[1, :, DH:], gk2), (grads.at[2], gv),
        ))
    ]
    for move in moves:
        move.start()
    for move in moves:
        move.wait()


def per_device(*arrays):
    q1, q2, k1, k2, v, o1, o2, totals, lam, gain, cot, block_of = arrays
    flat = lambda a: a.reshape(ROWS, a.shape[-1])
    hbm = pl.BlockSpec(memory_space=pltpu.HBM)
    vmem, smem = pl.BlockSpec(memory_space=pltpu.VMEM), pl.BlockSpec(memory_space=pltpu.SMEM)
    copies = 96
    shape = lambda width: jax.ShapeDtypeStruct((ROWS, width), BF16)
    grads = pl.pallas_call(
        kernel,
        out_shape=pltpu.VMEM((3, ROWS, DV), BF16),
        in_specs=[hbm] * 8 + [smem] + [hbm] * 3,
        out_specs=vmem,
        scratch_shapes=[
            pltpu.VMEM((ROWS, DV), BF16),
            pltpu.VMEM((ROWS, DV), BF16),
            pltpu.VMEM((1, 2, 2, HALF), F32),
            pltpu.VMEM((1, DV), F32),
            pltpu.VMEM((16, NU, DV), BF16),
            pltpu.SMEM((128,), jnp.int32),
            pltpu.SemaphoreType.DMA((11,)),
            pltpu.VMEM((NU, 16, DV), BF16),
            pltpu.VMEM((NU, 16, DV), BF16),
            pltpu.VMEM((8, ROWS, 2 * DH), BF16),
            pltpu.VMEM((8, GROWS, DV), BF16),
            pltpu.VMEM((8, ROWS, 2 * DH), BF16),
            pltpu.VMEM((8, ROWS, DV), BF16),
            pltpu.VMEM((2, 2, 8, 4 * HALF), F32),
            pltpu.VMEM((2, 2, 8, 4 * HALF), jnp.int32),
            pltpu.VMEM((8, ROWS, ROWS), jnp.int32),
            pltpu.VMEM((8, ROWS, 2 * DH), F32),
            pltpu.VMEM((8, ROWS, 2 * DH), F32),
            pltpu.VMEM((8, ROWS, DV), F32),
            pltpu.VMEM((16, ROWS, DV), BF16),
            pltpu.VMEM((16, ROWS, DV), BF16),
            pltpu.VMEM((6, ROWS, 2 * DH), BF16),
            pltpu.VMEM((6, ROWS, 2 * DH), BF16),
            pltpu.VMEM((ROWS, 2 * DH), BF16),
            pltpu.VMEM((ROWS, 2 * DH), BF16),
            pltpu.SemaphoreType.DMA((copies,)),
            pltpu.SemaphoreType.DMA((copies,)),
        ],
        compiler_params=pltpu.CompilerParams(
            collective_id=0, has_side_effects=True, vmem_limit_bytes=56 * 1024 * 1024
        ),
    )(
        flat(q1), flat(q2), flat(k1), flat(k2), flat(v), flat(o1), flat(o2),
        totals, lam, gain, cot.reshape(16, NU, DV), block_of,
    )
    out = pl.pallas_call(
        finish,
        out_shape=[shape(DH)] * 4 + [shape(DV)],
        in_specs=[vmem],
        out_specs=[hbm] * 5,
        scratch_shapes=[pltpu.SemaphoreType.DMA((5,))],
        compiler_params=pltpu.CompilerParams(vmem_limit_bytes=4 * 1024 * 1024),
    )(grads)
    return tuple(g.reshape(2, HALF, 1, g.shape[-1]) for g in out)


def solution(mesh):
    rows = P("blk", None, "ulysses", None)
    in_specs = (rows,) * 7 + (
        P("ulysses", None, "blk", None),
        P("ulysses"),
        P("ulysses", None),
        P("blk", "ulysses", None, None),
        P(),
    )
    return jax.shard_map(
        per_device, mesh=mesh, in_specs=in_specs, out_specs=(rows,) * 5, check_vma=False
    )
```

```python
import functools
import math

import jax
import jax.numpy as jnp
from jax import lax
from jax.experimental import pallas as pl
from jax.experimental.pallas import tpu as pltpu
from jax.sharding import PartitionSpec as P

MESH = pl.DeviceIdType.MESH
NX, NZ, NY, NU = 4, 8, 2, 8
ROWS, DH, DV, HALF = 128, 128, 256, 64
GROWS = ROWS + 16
EPS = 1e-05
LOG2E = math.log2(math.e)
F32, BF16 = jnp.float32, jnp.bfloat16
PARTS = (slice(0, HALF), slice(HALF, ROWS))
G_PARTS = (slice(0, HALF), slice(HALF, GROWS))
KSLOT = {4: 0, 5: 1, 3: 2, 6: 3, 2: 4, 7: 5, 1: 6, 0: 7}
KFROM = {place: d for d, place in KSLOT.items()}


def qslot(dx, dy):
    return dx + (0 if dy else 4)


def dot(a, b, dims):
    return lax.dot_general(a, b, (dims, ((), ())), preferred_element_type=F32)


def split3(value):
    high = value.astype(BF16)
    rest = value - high.astype(F32)
    middle = rest.astype(BF16)
    low = (rest - middle.astype(F32)).astype(BF16)
    return high.astype(F32), middle.astype(F32), low.astype(F32)


def kernel(
    q1, q2, k1, k2, v, o1_in, o2_in, totals_in, lam_ref, gain_in, cot_in_hbm, block_in,
    grads_out,
    o1, o2, totals, gain, cot, block_of, local, cot_out, cot_in, qb, gb, kb, vb, stat, qpos, kpos, gq_sum, gk_sum, gv_sum,
    zs, zr, xs, xr, ys, yr, send, recv,
):
    u = lax.axis_index("ulysses")
    blk = lax.axis_index("blk")
    x, z, y = blk // (NZ * NY), (blk // NY) % NZ, blk % NY

    def at(nx, nz, ny):
        return {"blk": (lax.rem(nx, NX) * NZ + lax.rem(nz, NZ)) * NY + lax.rem(ny, NY)}

    up, down, across = at(x, z + 1, y), at(x, z + NZ - 1, y), at(x, z, y + 1)
    x_peers = {dx: at(x + dx, z, y) for dx in (2, 1, 3)}
    u_peers = {r: {"ulysses": lax.rem(u + r, NU)} for r in range(1, NU)}

    moves = {}

    def view(place):
        return place[0].at[place[1:]] if isinstance(place, tuple) else place

    def move(name):
        i, src, dst, device = moves[name]
        return pltpu.make_async_remote_copy(
            src_ref=view(src), dst_ref=view(dst), send_sem=send.at[i], recv_sem=recv.at[i],
            device_id=device, device_id_type=MESH,
        )

    def go(name, src, dst, device):
        moves[name] = (len(moves), src, dst, device)
        move(name).start()

    def arrived(name):
        move(name).wait_recv()

    settled = set()

    def settle(names):
        for name in names:
            if name not in settled:
                move(name).wait_send()
                settled.add(name)

    own_q, own_k = qslot(0, 0), KSLOT[0]
    loads = []
    for i, (src, dst) in enumerate((
        (cot_in_hbm, cot),
        (k1, kb.at[own_k, :, :DH]), (k2, kb.at[own_k, :, DH:]), (v, vb.at[own_k]),
        (q1, qb.at[own_q, :, :DH]), (q2, qb.at[own_q, :, DH:]),
        (o1_in, o1), (o2_in, o2), (totals_in, totals), (gain_in, gain),
            (block_in, block_of),
    )):
        load = pltpu.make_async_copy(src, dst, local.at[i])
        load.start()
        loads.append(load)
    first_load, *loads = loads
    barrier = pltpu.get_barrier_semaphore()
    partners = [across, *u_peers.values(), *x_peers.values(), up, down]
    for partner in partners:
        pl.semaphore_signal(barrier, inc=1, device_id=partner, device_id_type=MESH)

    first_load.wait()
    to_row = lax.broadcasted_iota(jnp.int32, (ROWS, ROWS), 0)
    from_row = lax.broadcasted_iota(jnp.int32, (ROWS, ROWS), 1)
    wanted = (to_row % 16) * 8 + to_row // 16
    order = jnp.where(from_row == wanted, 1.0, 0.0).astype(BF16)
    rows_in = cot[...].astype(F32).reshape(ROWS, DV).astype(BF16)
    by_head = dot(order, rows_in, ((1,), (0,))).astype(BF16).reshape(NU, 16, DV)
    cot_out[...] = by_head

    for load in loads:
        load.wait()
    lane = lax.broadcasted_iota(jnp.int32, (8, 4 * HALF), 1)
    for dy in range(NY):
        sources = [at(x + NX - dx, z, y + dy)["blk"] for dx in range(NX)]
        for half in range(2):
            starts = [block_of[2 * source + half] for source in sources]
            start = jnp.where(
                lane < 2 * HALF,
                jnp.where(lane < HALF, starts[0], starts[1]),
                jnp.where(lane < 3 * HALF, starts[2], starts[3]),
            )
            qpos[dy, half] = start * HALF + lane % HALF
    row = lax.broadcasted_iota(jnp.int32, (ROWS, ROWS), 0)
    for slot in range(NZ):
        source = at(x, z + NZ - KFROM[slot], y)["blk"]
        low, high = block_of[2 * source], block_of[2 * source + 1]
        kpos[slot] = jnp.where(row < HALF, low * HALF + row, high * HALF + row - HALF)
    gq_sum[...] = jnp.zeros_like(gq_sum)
    gk_sum[...] = jnp.zeros_like(gk_sum)
    gv_sum[...] = jnp.zeros_like(gv_sum)
    pl.semaphore_wait(barrier, len(partners))

    for r, device in u_peers.items():
        go(f"c{r}", (cot_out, lax.rem(u + r, NU)), (cot_in, u), device)
    for way, device, sign in (("u", up, 1), ("d", down, -1)):
        slot = KSLOT[sign % NZ]
        go(f"k{way}1", (kb, own_k), (kb, slot), device)
    for way, device, sign in (("u", up, 1), ("d", down, -1)):
        slot = KSLOT[sign % NZ]
        go(f"v{way}1", (vb, own_k), (vb, slot), device)
    go("qy", (qb, own_q), (qb, qslot(0, 1)), across)
    for dx, device in x_peers.items():
        go(f"q{dx}", (qb, own_q), (qb, qslot(dx, 0)), device)

    def pass_on(hop, kinds):
        for kind, way, device, sign in kinds:
            arrived(f"{kind}{way}{hop}")
            held = {"k": kb, "v": vb}[kind]
            here, there = KSLOT[sign * hop % NZ], KSLOT[sign * (hop + 1) % NZ]
            go(f"{kind}{way}{hop + 1}", (held, here), (held, there), device)

    both = [(kind, way, device, sign) for kind in "kv" for way, device, sign in (("u", up, 1), ("d", down, -1))]
    cot_in[u] = cot_out[u]
    pass_on(1, both)
    for r in u_peers:
        arrived(f"c{r}")
    lam = lam_ref[0]
    parts = cot_in[...].astype(F32)
    grad_y = jnp.concatenate(
        [parts[w, s * 8 : s * 8 + 8] for s in range(2) for w in range(NU)], axis=0
    )
    first_out, second_out = o1[...].astype(F32), o2[...].astype(F32)
    combined = first_out - lam * second_out
    inv_rms = lax.rsqrt(jnp.mean(combined * combined, axis=-1, keepdims=True) + EPS)
    gained = gain[...] * grad_y
    centre = jnp.mean(combined * gained, axis=-1, keepdims=True)
    grad_out = (inv_rms * (gained - combined * inv_rms * inv_rms * centre)).astype(BF16)
    gb[own_q, :ROWS] = grad_out
    wide = grad_out.astype(F32)
    dot_one = jnp.sum(wide * first_out, axis=-1, keepdims=True)
    dot_two = jnp.sum(wide * second_out, axis=-1, keepdims=True)
    row_one = jnp.broadcast_to(dot_one, (ROWS, ROWS)).T[:1]
    row_two = jnp.broadcast_to(dot_two, (ROWS, ROWS)).T[:1]
    log_lam = jnp.log2(jnp.full((1, ROWS), lam, F32))
    total_one = jnp.concatenate([totals[0, 0, :1], totals[0, 0, 1:]], axis=1) * LOG2E
    total_two = jnp.concatenate([totals[0, 1, :1], totals[0, 1, 1:]], axis=1) * LOG2E
    stats = jnp.concatenate([total_one, total_two - log_lam, row_one, row_two], axis=0)
    coded = jnp.concatenate([*split3(stats), jnp.zeros((4, ROWS), F32)], axis=0)
    gb[own_q, ROWS:] = jnp.concatenate([coded, jnp.zeros((16, ROWS), F32)], axis=1).astype(BF16)

    for part, rows in enumerate(G_PARTS):
        go(f"gy{part}", (gb, own_q, rows), (gb, qslot(0, 1), rows), across)
    for dx, device in x_peers.items():
        go(f"g{dx}", (gb, own_q), (gb, qslot(dx, 0)), device)

    pass_on(2, both[:2])
    arrived("qy")
    for dx, device in x_peers.items():
        go(f"p{dx}", (qb, qslot(0, 1)), (qb, qslot(dx, 1)), device)
    pass_on(2, both[2:])

    scale = 1.0 / math.sqrt(DH)

    def unpack_stats(dy):
        whole = []
        for dx in range(NX):
            coded = gb[qslot(dx, dy), ROWS:, :ROWS].astype(F32)
            whole.append(coded[0:4] + coded[4:8] + coded[8:12])
        for half in range(2):
            part = slice(half * HALF, half * HALF + HALF)
            for side in range(2):
                pair = [w[:, part] for w in whole[2 * side : 2 * side + 2]]
                stat[dy, half, 0:4, side * ROWS : side * ROWS + ROWS] = jnp.concatenate(pair, axis=1)

    far, near, first = ((1,), (1,)), ((1,), (0,)), ((0,), (0,))

    def scores(keys, values, queries, grads):
        return (
            dot(keys[:, :DH], queries[:, :DH], far),
            dot(keys[:, DH:], queries[:, DH:], far),
            dot(values, grads, far),
        )

    def weights(raw, numbers, places, query_places):
        one, two, attn = raw
        seen = jnp.concatenate([places, places], axis=1) <= query_places
        one = one * (scale * LOG2E) - numbers[0:1]
        two = two * (scale * LOG2E) - numbers[1:2]
        prob_one = jnp.exp2(jnp.where(seen, one, -jnp.inf))
        prob_two = jnp.exp2(jnp.where(seen, two, -jnp.inf))
        grad_one = (prob_one * (attn - numbers[2:3])).astype(BF16)
        grad_two = (prob_two * (numbers[3:4] - attn)).astype(BF16)
        return grad_one, grad_two, (prob_one - prob_two).astype(BF16)

    def tile(i):
        early = i < 4
        dy = jnp.where(early, 0, 1)
        pair = pl.ds(2 * jnp.where(early, 3 - i, i - 4), 2)
        four = pl.ds(jnp.where(early, 4, 0), 4)
        keys = kb[pair].reshape(2 * ROWS, 2 * DH)
        values = vb[pair].reshape(2 * ROWS, DV)
        low_keys = kb[pair, :HALF].reshape(ROWS, 2 * DH)
        low_values = vb[pair, :HALF].reshape(ROWS, DV)
        queries = qb[four, HALF:].reshape(4 * HALF, 2 * DH)
        grads = gb[four, HALF:ROWS].reshape(4 * HALF, DV)
        low_queries = qb[four, :HALF].reshape(4 * HALF, 2 * DH)
        low_grads = gb[four, :HALF].reshape(4 * HALF, DV)
        high_raw = scores(keys, values, queries, grads)
        low_raw = scores(low_keys, low_values, low_queries, low_grads)
        one, two, mix = weights(high_raw, stat[dy, 1], kpos[pair].reshape(2 * ROWS, ROWS), qpos[dy, 1, :1])
        low_one, low_two, low_mix = weights(
            low_raw, stat[dy, 0], kpos[pair, :HALF].reshape(ROWS, ROWS), qpos[dy, 0, :1]
        )
        gq_sum[four, HALF:, :DH] += dot(one, keys[:, :DH], first).reshape(4, HALF, DH)
        gq_sum[four, HALF:, DH:] += dot(two, keys[:, DH:], first).reshape(4, HALF, DH)
        nothing = jnp.zeros((ROWS, DH), BF16)
        apart = jnp.concatenate(
            [
                jnp.concatenate([low_keys[:, :DH], nothing], axis=1),
                jnp.concatenate([nothing, low_keys[:, DH:]], axis=1),
            ],
            axis=0,
        )
        stacked = jnp.concatenate([low_one, low_two], axis=0)
        gq_sum[four, :HALF] += dot(stacked, apart, first).reshape(4, HALF, 2 * DH)
        gk_sum[pair, :, :DH] += dot(one, queries[:, :DH], near).reshape(2, ROWS, DH)
        gk_sum[pair, :, DH:] += dot(two, queries[:, DH:], near).reshape(2, ROWS, DH)
        gv_sum[pair] += dot(mix, grads, near).reshape(2, ROWS, DV)
        gk_sum[pair, :HALF, :DH] += dot(low_one, low_queries[:, :DH], near).reshape(2, HALF, DH)
        gk_sum[pair, :HALF, DH:] += dot(low_two, low_queries[:, DH:], near).reshape(2, HALF, DH)
        gv_sum[pair, :HALF] += dot(low_mix, low_grads, near).reshape(2, HALF, DV)

    total = {"k": gk_sum, "v": gv_sum}

    spot = {"u": 0, "d": 1}

    def place(kind, way, d):
        return {"k": 0, "v": 1}[kind] + 2 * spot[way] + 4 * (d - 1)

    def pass_sum(kind, way, d, joined, part):
        rows = PARTS[part]
        value = total[kind][KSLOT[(-d if way == "u" else d) % NZ], rows]
        if joined:
            arrived(f"r{kind}{way}{d + 1}{part}")
            value = value + zr[place(kind, way, d + 1), rows].astype(F32)
        i = place(kind, way, d)
        zs[i, rows] = value.astype(BF16)
        go(f"r{kind}{way}{d}{part}", (zs, i, rows), (zr, i, rows), up if way == "u" else down)

    def pass_sums(kinds, d, joined):
        for part in range(len(PARTS)):
            for kind, way in zip(kinds, "ud"):
                if kind in "kv":
                    pass_sum(kind, way, d, joined, part)

    def send_queries(dy, sends, first_at):
        for part, rows in enumerate(PARTS):
            for dx in (2, 1, 3):
                i = dx + first_at
                xs[i, rows] = gq_sum[qslot(dx, dy), rows].astype(BF16)
                go(f"{sends}{dx}{part}", (xs, i, rows), (xr, i, rows), x_peers[NX - dx])

    def step(i, carry):
        @pl.when(i == 0)
        def _():
            pass_on(3, both[:1])
            for dx in x_peers:
                arrived(f"q{dx}")
                arrived(f"g{dx}")
            for part, rows in enumerate(G_PARTS):
                arrived(f"gy{part}")
                for dx, device in x_peers.items():
                    go(f"h{dx}{part}", (gb, qslot(0, 1), rows), (gb, qslot(dx, 1), rows), device)
            unpack_stats(0)
            pass_on(3, both[3:])

        @pl.when(i == 2)
        def _():
            arrived("vu3")
            arrived("kd3")

        @pl.when(i == 3)
        def _():
            arrived("ku4")
            arrived("vd4")

        @pl.when(i == 4)
        def _():
            for dx in x_peers:
                arrived(f"p{dx}")
                for part in range(len(G_PARTS)):
                    arrived(f"h{dx}{part}")
            unpack_stats(1)

        @pl.when(i == 5)
        def _():
            pass_sums("kv", 4, False)
            pass_sums("v-", 3, False)

        @pl.when(i == 6)
        def _():
            pass_sums("-k", 3, False)
            send_queries(0, "t", 2)

        tile(i)
        return carry

    lax.fori_loop(0, 8, step, 0)
    before = list(moves)
    send_queries(1, "s", -1)
    settle(before[: len(before) // 2])
    pass_sums("kv", 3, True)
    settle(before)
    pass_sums("vk", 2, True)
    for part, rows in enumerate(PARTS):
        value = gq_sum[qslot(0, 1), rows]
        for dx in (1, 3, 2):
            arrived(f"s{dx}{part}")
            value = value + xr[dx - 1, rows].astype(F32)
        ys[rows] = value.astype(BF16)
        go(f"sy{part}", (ys, rows), (yr, rows), across)
    pass_sums("kv", 2, True)
    pass_sums("vk", 1, True)
    for part, rows in enumerate(PARTS):
        value = gq_sum[qslot(0, 0), rows]
        for dx in range(1, NX):
            arrived(f"t{dx}{part}")
            value = value + xr[dx + 2, rows].astype(F32)
        gq_sum[qslot(0, 0), rows] = value
    pass_sums("kv", 1, True)
    for part, rows in enumerate(PARTS):
        for kind in "vk":
            value = total[kind][KSLOT[0], rows]
            for way in "ud":
                arrived(f"r{kind}{way}1{part}")
                value = value + zr[place(kind, way, 1), rows].astype(F32)
            if kind == "k":
                grads_out[1, rows] = (value * scale).astype(BF16)
            else:
                grads_out[2, rows] = value.astype(BF16)
    settle(list(moves))
    for part, rows in enumerate(PARTS):
        arrived(f"sy{part}")
        value = (gq_sum[qslot(0, 0), rows] + yr[rows].astype(F32)) * scale
        grads_out[0, rows] = value.astype(BF16)


def finish(grads, gq1, gq2, gk1, gk2, gv, done):
    moves = [
        pltpu.make_async_copy(src, dst, done.at[i])
        for i, (src, dst) in enumerate((
            (grads.at[0, :, :DH], gq1), (grads.at[0, :, DH:], gq2),
            (grads.at[1, :, :DH], gk1), (grads.at[1, :, DH:], gk2), (grads.at[2], gv),
        ))
    ]
    for move in moves:
        move.start()
    for move in moves:
        move.wait()


def per_device(*arrays):
    q1, q2, k1, k2, v, o1, o2, totals, lam, gain, cot, block_of = arrays
    flat = lambda a: a.reshape(ROWS, a.shape[-1])
    hbm = pl.BlockSpec(memory_space=pltpu.HBM)
    vmem, smem = pl.BlockSpec(memory_space=pltpu.VMEM), pl.BlockSpec(memory_space=pltpu.SMEM)
    copies = 96
    shape = lambda width: jax.ShapeDtypeStruct((ROWS, width), BF16)
    grads = pl.pallas_call(
        kernel,
        out_shape=pltpu.VMEM((3, ROWS, DV), BF16),
        in_specs=[hbm] * 8 + [smem] + [hbm] * 3,
        out_specs=vmem,
        scratch_shapes=[
            pltpu.VMEM((ROWS, DV), BF16),
            pltpu.VMEM((ROWS, DV), BF16),
            pltpu.VMEM((1, 2, 2, HALF), F32),
            pltpu.VMEM((1, DV), F32),
            pltpu.VMEM((16, NU, DV), BF16),
            pltpu.SMEM((128,), jnp.int32),
            pltpu.SemaphoreType.DMA((11,)),
            pltpu.VMEM((NU, 16, DV), BF16),
            pltpu.VMEM((NU, 16, DV), BF16),
            pltpu.VMEM((8, ROWS, 2 * DH), BF16),
            pltpu.VMEM((8, GROWS, DV), BF16),
            pltpu.VMEM((8, ROWS, 2 * DH), BF16),
            pltpu.VMEM((8, ROWS, DV), BF16),
            pltpu.VMEM((2, 2, 8, 4 * HALF), F32),
            pltpu.VMEM((2, 2, 8, 4 * HALF), jnp.int32),
            pltpu.VMEM((8, ROWS, ROWS), jnp.int32),
            pltpu.VMEM((8, ROWS, 2 * DH), F32),
            pltpu.VMEM((8, ROWS, 2 * DH), F32),
            pltpu.VMEM((8, ROWS, DV), F32),
            pltpu.VMEM((16, ROWS, DV), BF16),
            pltpu.VMEM((16, ROWS, DV), BF16),
            pltpu.VMEM((6, ROWS, 2 * DH), BF16),
            pltpu.VMEM((6, ROWS, 2 * DH), BF16),
            pltpu.VMEM((ROWS, 2 * DH), BF16),
            pltpu.VMEM((ROWS, 2 * DH), BF16),
            pltpu.SemaphoreType.DMA((copies,)),
            pltpu.SemaphoreType.DMA((copies,)),
        ],
        compiler_params=pltpu.CompilerParams(
            collective_id=0, has_side_effects=True, vmem_limit_bytes=56 * 1024 * 1024
        ),
    )(
        flat(q1), flat(q2), flat(k1), flat(k2), flat(v), flat(o1), flat(o2),
        totals, lam, gain, cot.reshape(16, NU, DV), block_of,
    )
    out = pl.pallas_call(
        finish,
        out_shape=[shape(DH)] * 4 + [shape(DV)],
        in_specs=[vmem],
        out_specs=[hbm] * 5,
        scratch_shapes=[pltpu.SemaphoreType.DMA((5,))],
        compiler_params=pltpu.CompilerParams(vmem_limit_bytes=4 * 1024 * 1024),
    )(grads)
    return tuple(g.reshape(2, HALF, 1, g.shape[-1]) for g in out)


def solution(mesh):
    rows = P("blk", None, "ulysses", None)
    in_specs = (rows,) * 7 + (
        P("ulysses", None, "blk", None),
        P("ulysses"),
        P("ulysses", None),
        P("blk", "ulysses", None, None),
        P(),
    )
    return jax.shard_map(
        per_device, mesh=mesh, in_specs=in_specs, out_specs=(rows,) * 5, check_vma=False
    )
```

```python
import functools
import math

import jax
import jax.numpy as jnp
from jax import lax
from jax.experimental import pallas as pl
from jax.experimental.pallas import tpu as pltpu
from jax.sharding import PartitionSpec as P

MESH = pl.DeviceIdType.MESH
NX, NZ, NY, NU = 4, 8, 2, 8
ROWS, DH, DV, HALF = 128, 128, 256, 64
GROWS = ROWS + 16
EPS = 1e-05
LOG2E = math.log2(math.e)
F32, BF16 = jnp.float32, jnp.bfloat16
PARTS = (slice(0, HALF), slice(HALF, ROWS))
G_PARTS = (slice(0, HALF), slice(HALF, GROWS))
KSLOT = {4: 0, 5: 1, 3: 2, 6: 3, 2: 4, 7: 5, 1: 6, 0: 7}
KFROM = {place: d for d, place in KSLOT.items()}


def qslot(dx, dy):
    return dx + (0 if dy else 4)


def dot(a, b, dims):
    return lax.dot_general(a, b, (dims, ((), ())), preferred_element_type=F32)


def split3(value):
    high = value.astype(BF16)
    rest = value - high.astype(F32)
    middle = rest.astype(BF16)
    low = (rest - middle.astype(F32)).astype(BF16)
    return high.astype(F32), middle.astype(F32), low.astype(F32)


def kernel(
    q1, q2, k1, k2, v, o1_in, o2_in, totals_in, lam_ref, gain_in, cot_in_hbm, block_in,
    grads_out,
    o1, o2, totals, gain, cot, block_of, local, cot_out, cot_in, qb, gb, kb, vb, stat, qpos, kpos, gq_sum, gk_sum, gv_sum,
    zs, zr, xs, xr, ys, yr, send, recv,
):
    u = lax.axis_index("ulysses")
    blk = lax.axis_index("blk")
    x, z, y = blk // (NZ * NY), (blk // NY) % NZ, blk % NY

    def at(nx, nz, ny):
        return {"blk": (lax.rem(nx, NX) * NZ + lax.rem(nz, NZ)) * NY + lax.rem(ny, NY)}

    up, down, across = at(x, z + 1, y), at(x, z + NZ - 1, y), at(x, z, y + 1)
    x_peers = {dx: at(x + dx, z, y) for dx in (2, 1, 3)}
    u_peers = {r: {"ulysses": lax.rem(u + r, NU)} for r in range(1, NU)}

    moves = {}

    def view(place):
        return place[0].at[place[1:]] if isinstance(place, tuple) else place

    def move(name):
        i, src, dst, device = moves[name]
        return pltpu.make_async_remote_copy(
            src_ref=view(src), dst_ref=view(dst), send_sem=send.at[i], recv_sem=recv.at[i],
            device_id=device, device_id_type=MESH,
        )

    def go(name, src, dst, device):
        moves[name] = (len(moves), src, dst, device)
        move(name).start()

    def arrived(name):
        move(name).wait_recv()

    settled = set()

    def settle(names):
        for name in names:
            if name not in settled:
                move(name).wait_send()
                settled.add(name)

    own_q, own_k = qslot(0, 0), KSLOT[0]
    loads = []
    for i, (src, dst) in enumerate((
        (cot_in_hbm, cot),
        (k1, kb.at[own_k, :, :DH]), (k2, kb.at[own_k, :, DH:]), (v, vb.at[own_k]),
        (q1, qb.at[own_q, :, :DH]), (q2, qb.at[own_q, :, DH:]),
        (o1_in, o1), (o2_in, o2), (totals_in, totals), (gain_in, gain),
            (block_in, block_of),
    )):
        load = pltpu.make_async_copy(src, dst, local.at[i])
        load.start()
        loads.append(load)
    first_load, *loads = loads
    barrier = pltpu.get_barrier_semaphore()
    partners = [across, *u_peers.values(), *x_peers.values(), up, down]
    for partner in partners:
        pl.semaphore_signal(barrier, inc=1, device_id=partner, device_id_type=MESH)

    first_load.wait()
    to_row = lax.broadcasted_iota(jnp.int32, (ROWS, ROWS), 0)
    from_row = lax.broadcasted_iota(jnp.int32, (ROWS, ROWS), 1)
    wanted = (to_row % 16) * 8 + to_row // 16
    order = jnp.where(from_row == wanted, 1.0, 0.0).astype(BF16)
    rows_in = cot[...].astype(F32).reshape(ROWS, DV).astype(BF16)
    by_head = dot(order, rows_in, ((1,), (0,))).astype(BF16).reshape(NU, 16, DV)
    cot_out[...] = by_head

    for load in loads:
        load.wait()
    pl.semaphore_wait(barrier, len(partners))

    for r, device in u_peers.items():
        go(f"c{r}", (cot_out, lax.rem(u + r, NU)), (cot_in, u), device)
    for way, device, sign in (("u", up, 1), ("d", down, -1)):
        slot = KSLOT[sign % NZ]
        go(f"k{way}1", (kb, own_k), (kb, slot), device)
    for way, device, sign in (("u", up, 1), ("d", down, -1)):
        slot = KSLOT[sign % NZ]
        go(f"v{way}1", (vb, own_k), (vb, slot), device)
    go("qy", (qb, own_q), (qb, qslot(0, 1)), across)
    for dx, device in x_peers.items():
        go(f"q{dx}", (qb, own_q), (qb, qslot(dx, 0)), device)

    lane = lax.broadcasted_iota(jnp.int32, (8, 4 * HALF), 1)
    for dy in range(NY):
        sources = [at(x + NX - dx, z, y + dy)["blk"] for dx in range(NX)]
        for half in range(2):
            starts = [block_of[2 * source + half] for source in sources]
            start = jnp.where(
                lane < 2 * HALF,
                jnp.where(lane < HALF, starts[0], starts[1]),
                jnp.where(lane < 3 * HALF, starts[2], starts[3]),
            )
            qpos[dy, half] = start * HALF + lane % HALF
    row = lax.broadcasted_iota(jnp.int32, (ROWS, ROWS), 0)
    for slot in range(NZ):
        source = at(x, z + NZ - KFROM[slot], y)["blk"]
        low, high = block_of[2 * source], block_of[2 * source + 1]
        kpos[slot] = jnp.where(row < HALF, low * HALF + row, high * HALF + row - HALF)
    gq_sum[...] = jnp.zeros_like(gq_sum)
    gk_sum[...] = jnp.zeros_like(gk_sum)
    gv_sum[...] = jnp.zeros_like(gv_sum)
    def pass_on(hop, kinds):
        for kind, way, device, sign in kinds:
            arrived(f"{kind}{way}{hop}")
            held = {"k": kb, "v": vb}[kind]
            here, there = KSLOT[sign * hop % NZ], KSLOT[sign * (hop + 1) % NZ]
            go(f"{kind}{way}{hop + 1}", (held, here), (held, there), device)

    both = [(kind, way, device, sign) for kind in "kv" for way, device, sign in (("u", up, 1), ("d", down, -1))]
    cot_in[u] = cot_out[u]
    pass_on(1, both)
    for r in u_peers:
        arrived(f"c{r}")
    lam = lam_ref[0]
    parts = cot_in[...].astype(F32)
    grad_y = jnp.concatenate(
        [parts[w, s * 8 : s * 8 + 8] for s in range(2) for w in range(NU)], axis=0
    )
    first_out, second_out = o1[...].astype(F32), o2[...].astype(F32)
    combined = first_out - lam * second_out
    inv_rms = lax.rsqrt(jnp.mean(combined * combined, axis=-1, keepdims=True) + EPS)
    gained = gain[...] * grad_y
    centre = jnp.mean(combined * gained, axis=-1, keepdims=True)
    grad_out = (inv_rms * (gained - combined * inv_rms * inv_rms * centre)).astype(BF16)
    gb[own_q, :ROWS] = grad_out
    wide = grad_out.astype(F32)
    dot_one = jnp.sum(wide * first_out, axis=-1, keepdims=True)
    dot_two = jnp.sum(wide * second_out, axis=-1, keepdims=True)
    row_one = jnp.broadcast_to(dot_one, (ROWS, ROWS)).T[:1]
    row_two = jnp.broadcast_to(dot_two, (ROWS, ROWS)).T[:1]
    log_lam = jnp.log2(jnp.full((1, ROWS), lam, F32))
    total_one = jnp.concatenate([totals[0, 0, :1], totals[0, 0, 1:]], axis=1) * LOG2E
    total_two = jnp.concatenate([totals[0, 1, :1], totals[0, 1, 1:]], axis=1) * LOG2E
    stats = jnp.concatenate([total_one, total_two - log_lam, row_one, row_two], axis=0)
    coded = jnp.concatenate([*split3(stats), jnp.zeros((4, ROWS), F32)], axis=0)
    gb[own_q, ROWS:] = jnp.concatenate([coded, jnp.zeros((16, ROWS), F32)], axis=1).astype(BF16)

    for part, rows in enumerate(G_PARTS):
        go(f"gy{part}", (gb, own_q, rows), (gb, qslot(0, 1), rows), across)
    for dx, device in x_peers.items():
        go(f"g{dx}", (gb, own_q), (gb, qslot(dx, 0)), device)

    pass_on(2, both[:2])
    arrived("qy")
    for dx, device in x_peers.items():
        go(f"p{dx}", (qb, qslot(0, 1)), (qb, qslot(dx, 1)), device)
    pass_on(2, both[2:])

    scale = 1.0 / math.sqrt(DH)

    def unpack_stats(dy):
        whole = []
        for dx in range(NX):
            coded = gb[qslot(dx, dy), ROWS:, :ROWS].astype(F32)
            whole.append(coded[0:4] + coded[4:8] + coded[8:12])
        for half in range(2):
            part = slice(half * HALF, half * HALF + HALF)
            for side in range(2):
                pair = [w[:, part] for w in whole[2 * side : 2 * side + 2]]
                stat[dy, half, 0:4, side * ROWS : side * ROWS + ROWS] = jnp.concatenate(pair, axis=1)

    far, near, first = ((1,), (1,)), ((1,), (0,)), ((0,), (0,))

    def scores(keys, values, queries, grads):
        return (
            dot(keys[:, :DH], queries[:, :DH], far),
            dot(keys[:, DH:], queries[:, DH:], far),
            dot(values, grads, far),
        )

    def weights(raw, numbers, places, query_places):
        one, two, attn = raw
        seen = jnp.concatenate([places, places], axis=1) <= query_places
        one = one * (scale * LOG2E) - numbers[0:1]
        two = two * (scale * LOG2E) - numbers[1:2]
        prob_one = jnp.exp2(jnp.where(seen, one, -jnp.inf))
        prob_two = jnp.exp2(jnp.where(seen, two, -jnp.inf))
        grad_one = (prob_one * (attn - numbers[2:3])).astype(BF16)
        grad_two = (prob_two * (numbers[3:4] - attn)).astype(BF16)
        return grad_one, grad_two, (prob_one - prob_two).astype(BF16)

    def tile(i):
        early = i < 4
        dy = jnp.where(early, 0, 1)
        pair = pl.ds(2 * jnp.where(early, 3 - i, i - 4), 2)
        four = pl.ds(jnp.where(early, 4, 0), 4)
        keys = kb[pair].reshape(2 * ROWS, 2 * DH)
        values = vb[pair].reshape(2 * ROWS, DV)
        low_keys = kb[pair, :HALF].reshape(ROWS, 2 * DH)
        low_values = vb[pair, :HALF].reshape(ROWS, DV)
        queries = qb[four, HALF:].reshape(4 * HALF, 2 * DH)
        grads = gb[four, HALF:ROWS].reshape(4 * HALF, DV)
        low_queries = qb[four, :HALF].reshape(4 * HALF, 2 * DH)
        low_grads = gb[four, :HALF].reshape(4 * HALF, DV)
        high_raw = scores(keys, values, queries, grads)
        low_raw = scores(low_keys, low_values, low_queries, low_grads)
        one, two, mix = weights(high_raw, stat[dy, 1], kpos[pair].reshape(2 * ROWS, ROWS), qpos[dy, 1, :1])
        low_one, low_two, low_mix = weights(
            low_raw, stat[dy, 0], kpos[pair, :HALF].reshape(ROWS, ROWS), qpos[dy, 0, :1]
        )
        gq_sum[four, HALF:, :DH] += dot(one, keys[:, :DH], first).reshape(4, HALF, DH)
        gq_sum[four, HALF:, DH:] += dot(two, keys[:, DH:], first).reshape(4, HALF, DH)
        nothing = jnp.zeros((ROWS, DH), BF16)
        apart = jnp.concatenate(
            [
                jnp.concatenate([low_keys[:, :DH], nothing], axis=1),
                jnp.concatenate([nothing, low_keys[:, DH:]], axis=1),
            ],
            axis=0,
        )
        stacked = jnp.concatenate([low_one, low_two], axis=0)
        gq_sum[four, :HALF] += dot(stacked, apart, first).reshape(4, HALF, 2 * DH)
        gk_sum[pair, :, :DH] += dot(one, queries[:, :DH], near).reshape(2, ROWS, DH)
        gk_sum[pair, :, DH:] += dot(two, queries[:, DH:], near).reshape(2, ROWS, DH)
        gv_sum[pair] += dot(mix, grads, near).reshape(2, ROWS, DV)
        gk_sum[pair, :HALF, :DH] += dot(low_one, low_queries[:, :DH], near).reshape(2, HALF, DH)
        gk_sum[pair, :HALF, DH:] += dot(low_two, low_queries[:, DH:], near).reshape(2, HALF, DH)
        gv_sum[pair, :HALF] += dot(low_mix, low_grads, near).reshape(2, HALF, DV)

    total = {"k": gk_sum, "v": gv_sum}

    spot = {"u": 0, "d": 1}

    def place(kind, way, d):
        return {"k": 0, "v": 1}[kind] + 2 * spot[way] + 4 * (d - 1)

    def pass_sum(kind, way, d, joined, part):
        rows = PARTS[part]
        value = total[kind][KSLOT[(-d if way == "u" else d) % NZ], rows]
        if joined:
            arrived(f"r{kind}{way}{d + 1}{part}")
            value = value + zr[place(kind, way, d + 1), rows].astype(F32)
        i = place(kind, way, d)
        zs[i, rows] = value.astype(BF16)
        go(f"r{kind}{way}{d}{part}", (zs, i, rows), (zr, i, rows), up if way == "u" else down)

    def pass_sums(kinds, d, joined):
        for part in range(len(PARTS)):
            for kind, way in zip(kinds, "ud"):
                if kind in "kv":
                    pass_sum(kind, way, d, joined, part)

    def send_queries(dy, sends, first_at):
        for part, rows in enumerate(PARTS):
            for dx in (2, 1, 3):
                i = dx + first_at
                xs[i, rows] = gq_sum[qslot(dx, dy), rows].astype(BF16)
                go(f"{sends}{dx}{part}", (xs, i, rows), (xr, i, rows), x_peers[NX - dx])

    def step(i, carry):
        @pl.when(i == 0)
        def _():
            pass_on(3, both[:1])
            for dx in x_peers:
                arrived(f"q{dx}")
                arrived(f"g{dx}")
            for part, rows in enumerate(G_PARTS):
                arrived(f"gy{part}")
                for dx, device in x_peers.items():
                    go(f"h{dx}{part}", (gb, qslot(0, 1), rows), (gb, qslot(dx, 1), rows), device)
            unpack_stats(0)
            pass_on(3, both[3:])

        @pl.when(i == 2)
        def _():
            arrived("vu3")
            arrived("kd3")

        @pl.when(i == 3)
        def _():
            arrived("ku4")
            arrived("vd4")

        @pl.when(i == 4)
        def _():
            for dx in x_peers:
                arrived(f"p{dx}")
                for part in range(len(G_PARTS)):
                    arrived(f"h{dx}{part}")
            unpack_stats(1)

        @pl.when(i == 5)
        def _():
            pass_sums("kv", 4, False)
            pass_sums("v-", 3, False)

        @pl.when(i == 6)
        def _():
            pass_sums("-k", 3, False)

        tile(i)
        return carry

    lax.fori_loop(0, 8, step, 0)
    before = list(moves)
    send_queries(1, "s", -1)
    settle(before[: len(before) // 2])
    pass_sums("kv", 3, True)
    send_queries(0, "t", 2)
    settle(before)
    pass_sums("vk", 2, True)
    for part, rows in enumerate(PARTS):
        value = gq_sum[qslot(0, 1), rows]
        for dx in (1, 3, 2):
            arrived(f"s{dx}{part}")
            value = value + xr[dx - 1, rows].astype(F32)
        ys[rows] = value.astype(BF16)
        go(f"sy{part}", (ys, rows), (yr, rows), across)
    pass_sums("kv", 2, True)
    pass_sums("vk", 1, True)
    for part, rows in enumerate(PARTS):
        value = gq_sum[qslot(0, 0), rows]
        for dx in range(1, NX):
            arrived(f"t{dx}{part}")
            value = value + xr[dx + 2, rows].astype(F32)
        gq_sum[qslot(0, 0), rows] = value
    pass_sums("kv", 1, True)
    for part, rows in enumerate(PARTS):
        for kind in "vk":
            value = total[kind][KSLOT[0], rows]
            for way in "ud":
                arrived(f"r{kind}{way}1{part}")
                value = value + zr[place(kind, way, 1), rows].astype(F32)
            if kind == "k":
                grads_out[1, rows] = (value * scale).astype(BF16)
            else:
                grads_out[2, rows] = value.astype(BF16)
    settle(list(moves))
    for part, rows in enumerate(PARTS):
        arrived(f"sy{part}")
        value = (gq_sum[qslot(0, 0), rows] + yr[rows].astype(F32)) * scale
        grads_out[0, rows] = value.astype(BF16)


def finish(grads, gq1, gq2, gk1, gk2, gv, done):
    moves = [
        pltpu.make_async_copy(src, dst, done.at[i])
        for i, (src, dst) in enumerate((
            (grads.at[0, :, :DH], gq1), (grads.at[0, :, DH:], gq2),
            (grads.at[1, :, :DH], gk1), (grads.at[1, :, DH:], gk2), (grads.at[2], gv),
        ))
    ]
    for move in moves:
        move.start()
    for move in moves:
        move.wait()


def per_device(*arrays):
    q1, q2, k1, k2, v, o1, o2, totals, lam, gain, cot, block_of = arrays
    flat = lambda a: a.reshape(ROWS, a.shape[-1])
    hbm = pl.BlockSpec(memory_space=pltpu.HBM)
    vmem, smem = pl.BlockSpec(memory_space=pltpu.VMEM), pl.BlockSpec(memory_space=pltpu.SMEM)
    copies = 96
    shape = lambda width: jax.ShapeDtypeStruct((ROWS, width), BF16)
    grads = pl.pallas_call(
        kernel,
        out_shape=pltpu.VMEM((3, ROWS, DV), BF16),
        in_specs=[hbm] * 8 + [smem] + [hbm] * 3,
        out_specs=vmem,
        scratch_shapes=[
            pltpu.VMEM((ROWS, DV), BF16),
            pltpu.VMEM((ROWS, DV), BF16),
            pltpu.VMEM((1, 2, 2, HALF), F32),
            pltpu.VMEM((1, DV), F32),
            pltpu.VMEM((16, NU, DV), BF16),
            pltpu.SMEM((128,), jnp.int32),
            pltpu.SemaphoreType.DMA((11,)),
            pltpu.VMEM((NU, 16, DV), BF16),
            pltpu.VMEM((NU, 16, DV), BF16),
            pltpu.VMEM((8, ROWS, 2 * DH), BF16),
            pltpu.VMEM((8, GROWS, DV), BF16),
            pltpu.VMEM((8, ROWS, 2 * DH), BF16),
            pltpu.VMEM((8, ROWS, DV), BF16),
            pltpu.VMEM((2, 2, 8, 4 * HALF), F32),
            pltpu.VMEM((2, 2, 8, 4 * HALF), jnp.int32),
            pltpu.VMEM((8, ROWS, ROWS), jnp.int32),
            pltpu.VMEM((8, ROWS, 2 * DH), F32),
            pltpu.VMEM((8, ROWS, 2 * DH), F32),
            pltpu.VMEM((8, ROWS, DV), F32),
            pltpu.VMEM((16, ROWS, DV), BF16),
            pltpu.VMEM((16, ROWS, DV), BF16),
            pltpu.VMEM((6, ROWS, 2 * DH), BF16),
            pltpu.VMEM((6, ROWS, 2 * DH), BF16),
            pltpu.VMEM((ROWS, 2 * DH), BF16),
            pltpu.VMEM((ROWS, 2 * DH), BF16),
            pltpu.SemaphoreType.DMA((copies,)),
            pltpu.SemaphoreType.DMA((copies,)),
        ],
        compiler_params=pltpu.CompilerParams(
            collective_id=0, has_side_effects=True, vmem_limit_bytes=56 * 1024 * 1024
        ),
    )(
        flat(q1), flat(q2), flat(k1), flat(k2), flat(v), flat(o1), flat(o2),
        totals, lam, gain, cot.reshape(16, NU, DV), block_of,
    )
    out = pl.pallas_call(
        finish,
        out_shape=[shape(DH)] * 4 + [shape(DV)],
        in_specs=[vmem],
        out_specs=[hbm] * 5,
        scratch_shapes=[pltpu.SemaphoreType.DMA((5,))],
        compiler_params=pltpu.CompilerParams(vmem_limit_bytes=4 * 1024 * 1024),
    )(grads)
    return tuple(g.reshape(2, HALF, 1, g.shape[-1]) for g in out)


def solution(mesh):
    rows = P("blk", None, "ulysses", None)
    in_specs = (rows,) * 7 + (
        P("ulysses", None, "blk", None),
        P("ulysses"),
        P("ulysses", None),
        P("blk", "ulysses", None, None),
        P(),
    )
    return jax.shard_map(
        per_device, mesh=mesh, in_specs=in_specs, out_specs=(rows,) * 5, check_vma=False
    )
```
